256 devices in a mesh: slab: 32 (over y, x, core), batch: 8 (over z).
Axes of the slice: x: 4, y: 4, z: 8, core: 2. Of those that a mesh axis runs over, the one named last changes fastest.
Arguments:
- volume: bfloat16 [384, 384, 768], P('slab', 'batch'), may hold values from -6 to 6
- images: bfloat16 [1024, 384, 768], P('slab', 'batch'), may hold values from -6 to 6
- orient_ids: int32 [1024], P('slab'), may hold values from 0 to 7
- defocus_ids: int32 [1024], P('slab'), may hold values from 0 to 7
- ctf_tables: bfloat16 [8, 384, 384], P(None, 'batch'), may hold values from -1 to 1
- tilt_z: int32 [8], replicated, may hold values from -256 to 256
- tilt_x: int32 [8], replicated, may hold values from 192 to 256
Outputs:
- density_map: float32 [2, 384, 384, 384], P(None, 'slab', 'batch')
The draws below stay inside these ranges and needn't reach their ends.
Inputs may be any that keep to these rules, and one draw needn't show every extreme that they name: `orient_ids`: orientation of each particle, an index into tilt_z and tilt_x. `defocus_ids`: defocus class of each particle, an index into ctf_tables.
All inputs are finite; a program needn't handle non-finite values.
Results may differ from the reference program's by a relative error of at most 0.0012.
The reference program's roundings to bfloat16 on the way (of `updated`) count: a program that leaves them out, or rounds other values in their place, can miss the bound.
Values may be sent and summed in bfloat16 or wider, within the bound.
A program may use at most 128 MiB of HBM per device.

```python
import math
import jax
import jax.numpy as jnp
from jax import lax

BOX = 384
ORIENTS = 8
DEFOCI = 8
PARTS_SIZE = 1024


def set_ends(values, rng, smallest, largest):
    index_at = [jax.random.randint(jax.random.fold_in(rng, axis), (), 0, length) for axis, length in enumerate(values.shape)]
    longest = values.shape.index(max(values.shape))
    neighbour = index_at[:longest] + [(index_at[longest] + 1) % values.shape[longest]] + index_at[longest + 1:]
    return values.at[tuple(index_at)].set(smallest).at[tuple(neighbour)].set(largest)


def level_of(stream_key, shape, pieces, smallest, high):
    gain, own = 1.0, jax.random.fold_in(stream_key, 6)
    for axis_at, parts in pieces:
        steps = jnp.exp(jax.random.uniform(jax.random.fold_in(own, axis_at), (parts,), jnp.float32, smallest / len(pieces), high / len(pieces)))
        gain = gain * jnp.repeat(steps, shape[axis_at] // parts).reshape([-1 if axis == axis_at else 1 for axis in range(len(shape))])
    return gain


def bell_draw(own_key, shape, scale, limit, pieces=(), held_as=jnp.bfloat16):
    entries = jax.random.normal(own_key, shape, jnp.float32) * scale
    if len(pieces) > 0:
        entries = level_of(own_key, shape, pieces, -0.22, 0.18) * entries
    return jnp.clip(entries, min=-limit, max=limit).astype(held_as)


def setup_inputs(seed: int = 0) -> dict:
    arg_keys = jax.random.split(jax.random.key(seed), 8)
    volume = bell_draw(arg_keys[0], (BOX, BOX, 2 * BOX), 1.0, 6.0, ((0, 32), (1, 8)))
    images = bell_draw(arg_keys[1], (PARTS_SIZE, BOX, 2 * BOX), 1.0, 6.0, ((0, 32), (1, 8)))
    orient_ids = set_ends(jax.random.randint(arg_keys[2], (PARTS_SIZE,), 0, ORIENTS), jax.random.fold_in(arg_keys[2], 1), 0, ORIENTS - 1).astype(jnp.int32)
    defocus_ids = set_ends(jax.random.randint(arg_keys[3], (PARTS_SIZE,), 0, DEFOCI), jax.random.fold_in(arg_keys[3], 1), 0, DEFOCI - 1).astype(jnp.int32)
    ctf_tables = jnp.clip(jax.random.uniform(arg_keys[4], (DEFOCI, BOX, BOX), jnp.float32, -1.0, 1.0) * level_of(arg_keys[4], (DEFOCI, BOX, BOX), ((1, 8),), -0.4, 0.0), -1.0, 1.0).astype(jnp.bfloat16)
    tilt_z = set_ends(jax.random.randint(arg_keys[5], (ORIENTS,), -256, 257), jax.random.fold_in(arg_keys[5], 1), -256, 256).astype(jnp.int32)
    tilt_x = set_ends(jax.random.randint(arg_keys[6], (ORIENTS,), 192, 257), jax.random.fold_in(arg_keys[6], 1), 192, 256).astype(jnp.int32)
    return {"volume": volume, "images": images, "orient_ids": orient_ids, "defocus_ids": defocus_ids, "ctf_tables": ctf_tables, "tilt_z": tilt_z, "tilt_x": tilt_x}


TAU = 1.0

def interp_table(tilts, offset, extent, box_len):
    centre = box_len // 2
    column = jnp.arange(box_len, dtype=jnp.int32)
    plane_ids = offset + jnp.arange(extent, dtype=jnp.int32)
    position = centre * 256 + (column[None, :] - centre) * tilts[:, None]
    low_plane = position // 256
    fraction = (position - low_plane * 256).astype(jnp.float32) / 256.0
    low_hit = plane_ids[None, :, None] == low_plane[:, None, :]
    high_hit = plane_ids[None, :, None] == low_plane[:, None, :] + 1
    weights = jnp.where(low_hit, 1.0 - fraction[:, None, :], 0.0) + jnp.where(high_hit, fraction[:, None, :], 0.0)
    return weights.astype(jnp.bfloat16)

def dft_tables(box_len):
    indices = jnp.arange(box_len, dtype=jnp.int32)
    phases = indices[:, None] * indices[None, :] % box_len
    angles = phases.astype(jnp.float32) * (2.0 * math.pi / box_len)
    factor = 1.0 / math.sqrt(box_len)
    return ((jnp.cos(angles) * factor).astype(jnp.bfloat16), (jnp.sin(angles) * factor).astype(jnp.bfloat16))

def complex_pass(real_part, imag_part, cos_tab, sin_tab, form):
    cos_f = cos_tab.astype(jnp.float32)
    sin_f = sin_tab.astype(jnp.float32)
    real_f = real_part.astype(jnp.float32)
    imag_f = imag_part.astype(jnp.float32)
    out_real = jnp.einsum(form, real_f, cos_f) - jnp.einsum(form, imag_f, sin_f)
    out_imag = jnp.einsum(form, real_f, sin_f) + jnp.einsum(form, imag_f, cos_f)
    return (out_real, out_imag)

def reference(volume, images, orient_ids, defocus_ids, ctf_tables, tilt_z, tilt_x):
    box_len = volume.shape[0]
    orients = tilt_z.shape[0]
    depth_tab = interp_table(tilt_z, jnp.int32(0), box_len, box_len)
    width_tab = interp_table(tilt_x, jnp.int32(0), box_len, box_len)
    volume_cube = volume.reshape(box_len, box_len, 2, box_len)

    def project(tables):
        depth_w, width_w = tables
        width_f = width_w.astype(jnp.float32)

        def add_plane(running, record):
            z_plane, weights = record
            resampled = jnp.einsum('ycx,xk->yck', z_plane.astype(jnp.float32), width_f)
            return (running + resampled * weights.astype(jnp.float32)[None, None, :], None)
        start_value = jnp.zeros((box_len, 2, box_len), jnp.float32)
        return lax.scan(add_plane, start_value, (volume_cube, depth_w))[0]
    projection = lax.map(project, (depth_tab, width_tab))
    ctf_f = ctf_tables.astype(jnp.float32)

    def accumulate(state_pair, record):
        numer_sums, ctf_power = state_pair
        picture, orient, defocus = record
        ctf_row = ctf_f[defocus]
        mismatch = picture.reshape(box_len, 2, box_len).astype(jnp.float32) - ctf_row[:, None, :] * projection[orient]
        numer_sums = numer_sums.at[orient].add(ctf_row[:, None, :] * mismatch)
        ctf_power = ctf_power.at[orient].add(ctf_row * ctf_row)
        return ((numer_sums, ctf_power), None)
    start_sums = (jnp.zeros((orients, box_len, 2, box_len), jnp.float32), jnp.zeros((orients, box_len, box_len), jnp.float32))
    numer_sums, ctf_power = lax.scan(accumulate, start_sums, (images, orient_ids, defocus_ids))[0]
    width_f = width_tab.astype(jnp.float32)

    def rebuild(record):
        z_plane, depth_w = record
        depth_f = depth_w.astype(jnp.float32)
        operand = lax.optimization_barrier((depth_f[:, None, None, :] * numer_sums).astype(jnp.bfloat16)).astype(jnp.float32)
        numer_plane = jnp.einsum('oyck,oxk->ycx', operand, width_f)
        weight_op = lax.optimization_barrier((depth_f[:, None, :] * ctf_power).astype(jnp.bfloat16)).astype(jnp.float32)
        weight_plane = jnp.einsum('oyk,oxk->yx', weight_op, width_f)
        return (z_plane.astype(jnp.float32) + numer_plane / (weight_plane[:, None, :] + TAU)).astype(jnp.bfloat16)
    updated = lax.map(rebuild, (volume_cube, jnp.moveaxis(depth_tab, 1, 0)))
    cos_tab, sin_tab = dft_tables(box_len)

    def pass_x(z_plane):
        out_real, out_imag = complex_pass(z_plane[:, 0], z_plane[:, 1], cos_tab, sin_tab, 'yx,xn->yn')
        return jnp.stack([out_real, out_imag], axis=1).astype(jnp.bfloat16)

    def pass_y(z_plane):
        out_real, out_imag = complex_pass(z_plane[:, 0], z_plane[:, 1], cos_tab, sin_tab, 'yx,yn->nx')
        return jnp.stack([out_real, out_imag], axis=1).astype(jnp.bfloat16)

    def pass_z(column):
        out_real, out_imag = complex_pass(column[:, 0], column[:, 1], cos_tab, sin_tab, 'zx,zn->xn')
        return jnp.stack([out_real, out_imag], axis=0)
    along_x = lax.map(pass_x, updated)
    along_y = lax.map(pass_y, along_x)
    result = lax.map(pass_z, jnp.moveaxis(along_y, 1, 0))
    return jnp.moveaxis(result, 1, 0)
```

```python
import functools
import math

import jax
import jax.numpy as jnp
import numpy as np
from jax import lax
from jax.experimental import pallas as pl
from jax.experimental.pallas import tpu as pltpu
from jax.sharding import PartitionSpec as P

TAU = 1.0
BOX = 384
HALF = 192
ORI = 8
DEF = 8
NS = 32
NB = 8
ZL = BOX // NS
YL = BOX // NB
XL = BOX // NB
CH = 3
ZC = ZL // CH
PIECE = 24
CHIPS = NS // 2
LANES = 640
F32 = jnp.float32
BF16 = jnp.bfloat16
VMEM = pl.BlockSpec(memory_space=pltpu.VMEM)
SMEM = pl.BlockSpec(memory_space=pltpu.SMEM)
LIMIT = 50 * 1024 * 1024


def dft_tables():
    index = np.arange(BOX, dtype=np.int64)
    phases = (index[:, None] * index[None, :] % BOX).astype(np.float64)
    angles = phases * (2.0 * math.pi / BOX)
    factor = 1.0 / math.sqrt(BOX)
    return np.cos(angles) * factor, np.sin(angles) * factor


def pass_tables():
    cos, sin = dft_tables()
    x_tab = np.concatenate([cos, -sin], axis=0).T
    full = np.stack([np.stack([cos, sin], 1), np.stack([-sin, cos], 1)], 0)
    y_tab = full.reshape(2, NB, YL, 2, NS, ZL).transpose(4, 3, 5, 1, 0, 2).reshape(2 * BOX, 2 * BOX)
    z_tab = full.reshape(2, NS, ZL, 2, BOX).transpose(2, 0, 1, 3, 4).reshape(2 * BOX, 2 * BOX)
    return tuple(jnp.asarray(t.astype(np.float32), F32).astype(BF16) for t in (x_tab, y_tab, z_tab))


def sums_kernel(orient_ref, defocus_ref, image_ref, ctf_ref, sum_ref, count_ref):
    sum_ref[...] = jnp.zeros_like(sum_ref)
    row = lax.broadcasted_iota(jnp.int32, count_ref.shape, 0)
    lane = lax.broadcasted_iota(jnp.int32, count_ref.shape, 1)

    def step(p, count):
        orient, defocus = orient_ref[p], defocus_ref[p]
        ctf = ctf_ref[defocus].astype(F32)
        for h in range(2):
            cols = slice(h * BOX, (h + 1) * BOX)
            sum_ref[orient, :, cols] += ctf * image_ref[p, :, cols].astype(F32)
        return count + jnp.where((row == orient) & (lane == defocus), 1.0, 0.0)

    count_ref[...] = lax.fori_loop(0, image_ref.shape[0], step, jnp.zeros(count_ref.shape, F32))


def local_sums(orient_ids, defocus_ids, images, ctf_tables):
    return pl.pallas_call(
        sums_kernel,
        out_shape=(
            jax.ShapeDtypeStruct((ORI, YL, 2 * BOX), F32),
            jax.ShapeDtypeStruct((8, 128), F32),
        ),
        in_specs=[SMEM, SMEM, VMEM, VMEM],
        out_specs=(VMEM, VMEM),
        compiler_params=pltpu.CompilerParams(vmem_limit_bytes=LIMIT),
        name="local_sums",
    )(orient_ids, defocus_ids, images, ctf_tables)


def slab_copy(src, dst, send, recv, to):
    return pltpu.make_async_remote_copy(
        src_ref=src, dst_ref=dst, send_sem=send, recv_sem=recv,
        device_id={"slab": to}, device_id_type=pl.DeviceIdType.MESH,
    )


def reduce_kernel(
    sum_ref, count_ref, edge_ref,
    out_ref, counts_ref, halo_ref,
    pair_buf, piece_buf, part_buf, total_buf, count_buf, count_pair,
    pair_send, pair_recv, part_send, part_recv, gather_send, gather_recv, twin_send, twin_recv,
    count_send, count_recv, halo_send, halo_recv,
):
    me = lax.axis_index("slab")
    core = lax.rem(me, 2)
    chip = me // 2
    twin = me + 1 - 2 * core
    below = lax.rem(me + NS - 1, NS)
    above = lax.rem(me + 1, NS)
    outer = lax.rem(me + NS + 2 * core - 1, NS)

    def peer(d):
        return 2 * lax.rem(chip + d, CHIPS) + core

    barrier = pltpu.get_barrier_semaphore()
    pl.semaphore_signal(barrier, inc=1, device_id={"slab": twin}, device_id_type=pl.DeviceIdType.MESH)
    pl.semaphore_signal(barrier, inc=1, device_id={"slab": outer}, device_id_type=pl.DeviceIdType.MESH)

    def greet(d, _):
        pl.semaphore_signal(barrier, inc=1, device_id={"slab": peer(d)}, device_id_type=pl.DeviceIdType.MESH)
        return 0

    lax.fori_loop(1, CHIPS, greet, 0)
    pl.semaphore_wait(barrier, CHIPS + 1)

    rows = ORI * YL // 2
    keep = pl.multiple_of(rows * core, rows)
    give = pl.multiple_of(rows * (1 - core), rows)
    pair = slab_copy(sum_ref.at[pl.ds(give, rows)], pair_buf, pair_send, pair_recv, twin)
    pair.start()
    count_twin = slab_copy(count_ref, count_pair, count_send.at[0], count_recv.at[0], twin)
    count_twin.start()
    halo_up = slab_copy(edge_ref.at[1], halo_ref.at[0], halo_send.at[0], halo_recv.at[0], above)
    halo_up.start()
    halo_down = slab_copy(edge_ref.at[0], halo_ref.at[1], halo_send.at[1], halo_recv.at[1], below)
    halo_down.start()

    count_twin.wait()
    count_buf[0] = count_ref[...] + count_pair[...]

    def count_go(d, _):
        slab_copy(count_buf.at[0], count_buf.at[d], count_send.at[d], count_recv.at[d], peer(d)).start()
        return 0

    lax.fori_loop(1, CHIPS, count_go, 0)

    pair.wait()
    for j in range(CHIPS):
        r, c = PIECE * (j // 2), BOX * (j % 2)
        piece_buf[j] = (
            sum_ref[pl.ds(pl.multiple_of(keep + r, 8), PIECE), c : c + BOX] + pair_buf[r : r + PIECE, c : c + BOX]
        )

    def part_copy(d):
        to = lax.rem(chip + d, CHIPS)
        return slab_copy(piece_buf.at[to], part_buf.at[d], part_send.at[d], part_recv.at[d], peer(d))

    def part_go(d, _):
        part_copy(d).start()
        return 0

    lax.fori_loop(1, CHIPS, part_go, 0)

    def part_add(d, _):
        part_copy(d).wait()
        total_buf[...] += part_buf[d]
        return 0

    total_buf[...] = piece_buf[chip]
    lax.fori_loop(1, CHIPS, part_add, 0)

    def place(ref, which):
        r = pl.multiple_of(keep + PIECE * (which // 2), 8)
        c = pl.multiple_of(BOX * lax.rem(which, 2), 128)
        return ref.at[pl.ds(r, PIECE), pl.ds(c, BOX)]

    def gather_copy(d):
        return slab_copy(total_buf, place(out_ref, chip), gather_send.at[d], gather_recv.at[d], peer(d))

    def gather_go(d, _):
        gather_copy(d).start()
        return 0

    lax.fori_loop(1, CHIPS, gather_go, 0)
    own_r = pl.multiple_of(keep + PIECE * (chip // 2), 8)
    own_c = pl.multiple_of(BOX * lax.rem(chip, 2), 128)
    out_ref[pl.ds(own_r, PIECE), pl.ds(own_c, BOX)] = total_buf[...]

    def twin_copy(d):
        which = lax.rem(chip + CHIPS - d, CHIPS)
        return slab_copy(place(out_ref, which), place(out_ref, which), twin_send.at[d], twin_recv.at[d], twin)

    twin_copy(0).start()

    def gather_done(d, _):
        gather_copy(d).wait()
        twin_copy(d).start()
        return 0

    lax.fori_loop(1, CHIPS, gather_done, 0)

    def count_done(d, total):
        slab_copy(count_buf.at[0], count_buf.at[d], count_send.at[d], count_recv.at[d], peer(d)).wait()
        return total + count_buf[d]

    counts_ref[...] = lax.fori_loop(1, CHIPS, count_done, count_buf[0])
    halo_up.wait()
    halo_down.wait()

    def twin_done(d, _):
        twin_copy(d).wait()
        return 0

    lax.fori_loop(0, CHIPS, twin_done, 0)


def reduce_sums(sums, counts, edges):
    dma = pltpu.SemaphoreType.DMA
    return pl.pallas_call(
        reduce_kernel,
        out_shape=(
            jax.ShapeDtypeStruct((ORI * YL, 2 * BOX), F32),
            jax.ShapeDtypeStruct((8, 128), F32),
            jax.ShapeDtypeStruct((2, YL, 2 * BOX), BF16),
        ),
        in_specs=[VMEM] * 3,
        out_specs=(VMEM,) * 3,
        scratch_shapes=[
            pltpu.VMEM((ORI * YL // 2, 2 * BOX), F32),
            pltpu.VMEM((CHIPS, PIECE, BOX), F32),
            pltpu.VMEM((CHIPS, PIECE, BOX), F32),
            pltpu.VMEM((PIECE, BOX), F32),
            pltpu.VMEM((CHIPS, 8, 128), F32),
            pltpu.VMEM((8, 128), F32),
            dma(()), dma(()),
            dma((CHIPS,)), dma((CHIPS,)), dma((CHIPS,)), dma((CHIPS,)), dma((CHIPS,)), dma((CHIPS,)),
            dma((CHIPS,)), dma((CHIPS,)), dma((2,)), dma((2,)),
        ],
        compiler_params=pltpu.CompilerParams(vmem_limit_bytes=LIMIT, collective_id=0, has_side_effects=True),
        name="reduce_sums",
    )(sums, counts, edges)


def interp_row(tilt):
    column = lax.broadcasted_iota(jnp.int32, (1, BOX), 1)
    position = HALF * 256 + (column - HALF) * tilt
    low = position >> 8
    fraction = (position & 255).astype(F32) * (1.0 / 256.0)
    return low, fraction


def update_kernel(
    sum_ref, count_ref, halo_ref, vol_ref, ctf_ref, tz_ref, tx_ref, xtab_ref,
    out_ref,
    width, depth, numer, power, operand, paired,
):
    first = lax.axis_index("slab") * ZL - 1
    plane = lax.broadcasted_iota(jnp.int32, (16, BOX), 0) + first
    column = lax.broadcasted_iota(jnp.int32, (BOX, BOX), 0)
    for o in range(ORI):
        low, frac = interp_row(tz_ref[o])
        weights = jnp.where(plane == low, 1.0 - frac, 0.0) + jnp.where(plane == low + 1, frac, 0.0)
        depth[o] = jnp.where(plane < BOX, weights, 0.0)
        low, frac = interp_row(tx_ref[o])
        table = jnp.where(column == low, 1.0 - frac, 0.0) + jnp.where(column == low + 1, frac, 0.0)
        width[:, o * BOX : (o + 1) * BOX] = table.astype(BF16)
    ctf = ctf_ref[...].astype(F32)
    square = ctf * ctf
    for o in range(ORI):
        total = jnp.zeros((YL, BOX), F32)
        for d in range(DEF):
            total = total + count_ref[o : o + 1, d : d + 1] * square[d]
        power[o] = total
        for h in range(2):
            cols = slice(h * BOX, (h + 1) * BOX)
            stack = jnp.concatenate(
                [halo_ref[0, :, cols][None], vol_ref[:, :, cols], halo_ref[1, :, cols][None]], axis=0
            ).reshape((ZL + 2) * YL, BOX)
            seen = jnp.dot(stack, width[:, o * BOX : (o + 1) * BOX], preferred_element_type=F32)
            seen = seen.reshape(ZL + 2, YL, BOX)
            proj = jnp.zeros((YL, BOX), F32)
            for j in range(ZL + 2):
                proj = proj + depth[o, j : j + 1, :] * seen[j]
            numer[o, :, cols] = sum_ref[o * YL : (o + 1) * YL, cols] - total * proj
    for c in range(CH):
        for o in range(ORI):
            k = slice(o * BOX, (o + 1) * BOX)
            for zi in range(ZC):
                j = c * ZC + zi + 1
                w = depth[o, j : j + 1, :]
                for h in range(2):
                    r = (zi * 2 + h) * YL
                    operand[r : r + YL, k] = (w * numer[o, :, h * BOX : (h + 1) * BOX]).astype(BF16)
                r = (2 * ZC + zi) * YL
                operand[r : r + YL, k] = (w * power[o]).astype(BF16)
        back = lax.dot_general(
            operand[...], width[...], (((1,), (1,)), ((), ())), preferred_element_type=F32
        )
        for zi in range(ZC):
            weight = back[(2 * ZC + zi) * YL : (2 * ZC + zi + 1) * YL] + TAU
            parts = []
            for h in range(2):
                r = (zi * 2 + h) * YL
                old = vol_ref[c * ZC + zi, :, h * BOX : (h + 1) * BOX].astype(F32)
                parts.append((old + back[r : r + YL] / weight).astype(BF16))
            r = zi * 2 * YL
            paired[r : r + YL, :BOX] = parts[0]
            paired[r : r + YL, BOX:] = parts[1]
            paired[r + YL : r + 2 * YL, :BOX] = parts[1]
            paired[r + YL : r + 2 * YL, BOX:] = -parts[0]
        out_ref[c] = lax.dot_general(
            xtab_ref[...], paired[...], (((1,), (1,)), ((), ())), preferred_element_type=F32
        ).astype(BF16)


def update_volume(sums, counts, halo, volume, ctf_tables, tilt_z, tilt_x, x_tab):
    return pl.pallas_call(
        update_kernel,
        out_shape=jax.ShapeDtypeStruct((CH, BOX, ZC * 2 * YL), BF16),
        in_specs=[VMEM] * 5 + [SMEM] * 2 + [VMEM],
        out_specs=VMEM,
        scratch_shapes=[
            pltpu.VMEM((BOX, ORI * BOX), BF16),
            pltpu.VMEM((ORI, 16, BOX), F32),
            pltpu.VMEM((ORI, YL, 2 * BOX), F32),
            pltpu.VMEM((ORI, YL, BOX), F32),
            pltpu.VMEM((ZC * 3 * YL, ORI * BOX), BF16),
            pltpu.VMEM((ZC * 2 * YL, 2 * BOX), BF16),
        ],
        compiler_params=pltpu.CompilerParams(vmem_limit_bytes=LIMIT),
        name="update_volume",
    )(sums, counts, halo, volume, ctf_tables, tilt_z, tilt_x, x_tab)


def batch_kernel(in_ref, out_ref, send, recv, own):
    me = lax.axis_index("batch")

    def peer(d):
        return lax.rem(me + d, NB)

    barrier = pltpu.get_barrier_semaphore()
    for d in range(1, NB):
        pl.semaphore_signal(barrier, inc=1, device_id={"batch": peer(d)}, device_id_type=pl.DeviceIdType.MESH)
    pl.semaphore_wait(barrier, NB - 1)

    def copy(c, d):
        return pltpu.make_async_remote_copy(
            src_ref=in_ref.at[c, peer(d)], dst_ref=out_ref.at[c, me], send_sem=send.at[c, d], recv_sem=recv.at[c, d],
            device_id={"batch": peer(d)}, device_id_type=pl.DeviceIdType.MESH,
        )

    local = [pltpu.make_async_copy(in_ref.at[c, me], out_ref.at[c, me], own.at[c]) for c in range(CH)]
    for c in range(CH):
        for d in (4, 3, 5, 2, 6, 1, 7):
            copy(c, d).start()
        local[c].start()
    for c in range(CH):
        for d in range(1, NB):
            copy(c, d).wait()
        local[c].wait()


def batch_exchange(x):
    dma = pltpu.SemaphoreType.DMA
    return pl.pallas_call(
        batch_kernel,
        out_shape=jax.ShapeDtypeStruct(x.shape, x.dtype),
        in_specs=[VMEM],
        out_specs=VMEM,
        scratch_shapes=[dma((CH, NB)), dma((CH, NB)), dma((CH,))],
        compiler_params=pltpu.CompilerParams(vmem_limit_bytes=LIMIT, collective_id=1, has_side_effects=True),
        name="batch_exchange",
    )(x)


def ypass_kernel(in_ref, ytab_ref, out_ref, gathered):
    for z in range(ZL):
        lanes = slice((z % ZC) * 2 * YL, (z % ZC + 1) * 2 * YL)
        gathered[z * XL : (z + 1) * XL, :] = jnp.concatenate(
            [in_ref[z // ZC, b, :, lanes] for b in range(NB)], axis=1
        )
    out = lax.dot_general(ytab_ref[...], gathered[...], (((1,), (1,)), ((), ())), preferred_element_type=F32)
    out_ref[:, :, : ZL * XL] = out.astype(BF16).reshape(NS, 2 * ZL, ZL * XL)
    out_ref[:, :, ZL * XL :] = jnp.zeros((NS, 2 * ZL, LANES - ZL * XL), BF16)


def ypass(x, y_tab):
    return pl.pallas_call(
        ypass_kernel,
        out_shape=jax.ShapeDtypeStruct((NS, 2 * ZL, LANES), BF16),
        in_specs=[VMEM, VMEM],
        out_specs=VMEM,
        scratch_shapes=[pltpu.VMEM((ZL * XL, 2 * BOX), BF16)],
        compiler_params=pltpu.CompilerParams(vmem_limit_bytes=LIMIT),
        name="ypass",
    )(x, y_tab)


def slab_kernel(in_ref, out_ref, send, recv, own):
    me = lax.axis_index("slab")

    def peer(d):
        return lax.rem(me + d, NS)

    barrier = pltpu.get_barrier_semaphore()

    def greet(d, _):
        pl.semaphore_signal(barrier, inc=1, device_id={"slab": peer(d)}, device_id_type=pl.DeviceIdType.MESH)
        return 0

    lax.fori_loop(1, NS, greet, 0)
    pl.semaphore_wait(barrier, NS - 1)

    def copy(d):
        return slab_copy(in_ref.at[peer(d)], out_ref.at[me], send.at[d], recv.at[d], peer(d))

    def go(d, _):
        copy(d).start()
        return 0

    local = pltpu.make_async_copy(in_ref.at[me], out_ref.at[me], own)
    local.start()
    lax.fori_loop(1, NS, go, 0)

    def done(d, _):
        copy(d).wait()
        return 0

    lax.fori_loop(1, NS, done, 0)
    local.wait()


def slab_exchange(x):
    dma = pltpu.SemaphoreType.DMA
    return pl.pallas_call(
        slab_kernel,
        out_shape=jax.ShapeDtypeStruct(x.shape, x.dtype),
        in_specs=[VMEM],
        out_specs=VMEM,
        scratch_shapes=[dma((NS,)), dma((NS,)), dma(())],
        compiler_params=pltpu.CompilerParams(vmem_limit_bytes=LIMIT, collective_id=2, has_side_effects=True),
        name="slab_exchange",
    )(x)


def zpass_kernel(in_ref, ztab_ref, out_ref, wide, gathered):
    for t in range(LANES // 128):
        lanes = slice(t * 128, (t + 1) * 128)
        wide[t] = in_ref[:, :, lanes].astype(F32).reshape(NS * 2 * ZL, 128)
    for z in range(ZL):
        lane = z * XL
        t, off = lane // 128, lane % 128
        for h in range(2):
            blocks = []
            for y in range(ZL):
                rows = pl.ds(h * ZL + y, NS, 2 * ZL)
                if off + XL <= 128:
                    blocks.append(wide[t, rows, :][:, off : off + XL])
                else:
                    both = jnp.concatenate([wide[t, rows, :], wide[t + 1, rows, :]], axis=1)
                    blocks.append(both[:, off : off + XL])
            r = (z * 2 + h) * NS
            gathered[r : r + NS, :] = jnp.concatenate(blocks, axis=1).astype(BF16)
    out = lax.dot_general(gathered[...], ztab_ref[...], (((0,), (0,)), ((), ())), preferred_element_type=F32)
    out_ref[0] = out[:, :BOX]
    out_ref[1] = out[:, BOX:]


def zpass(x, z_tab):
    return pl.pallas_call(
        zpass_kernel,
        out_shape=jax.ShapeDtypeStruct((2, ZL * XL, BOX), F32),
        in_specs=[VMEM, VMEM],
        out_specs=VMEM,
        scratch_shapes=[
            pltpu.VMEM((LANES // 128, NS * 2 * ZL, 128), F32),
            pltpu.VMEM((2 * BOX, ZL * XL), BF16),
        ],
        compiler_params=pltpu.CompilerParams(vmem_limit_bytes=LIMIT),
        name="zpass",
    )(x, z_tab)


def local(volume, images, orient_ids, defocus_ids, ctf_tables, tilt_z, tilt_x):
    x_tab, y_tab, z_tab = pass_tables()
    sums, counts = local_sums(orient_ids, defocus_ids, images, ctf_tables)
    edges = jnp.stack([volume[0], volume[-1]])
    sums, counts, halo = reduce_sums(sums.reshape(ORI * YL, 2 * BOX), counts, edges)
    along_x = update_volume(sums, counts, halo, volume, ctf_tables, tilt_z, tilt_x, x_tab)
    pieces = batch_exchange(along_x.reshape(CH, NB, XL, ZC * 2 * YL))
    along_y = ypass(pieces, y_tab)
    pieces = slab_exchange(along_y)
    return zpass(pieces, z_tab).reshape(2, ZL, XL, BOX)


def solution(mesh):
    in_specs = (
        P("slab", "batch", None),
        P("slab", "batch", None),
        P("slab"),
        P("slab"),
        P(None, "batch", None),
        P(),
        P(),
    )
    out_specs = P(None, "slab", "batch", None)
    return jax.shard_map(local, mesh=mesh, in_specs=in_specs, out_specs=out_specs, check_vma=False)
```

```python
import functools
import math

import jax
import jax.numpy as jnp
import numpy as np
from jax import lax
from jax.experimental import pallas as pl
from jax.experimental.pallas import tpu as pltpu
from jax.sharding import PartitionSpec as P

TAU = 1.0
BOX = 384
HALF = 192
ORI = 8
DEF = 8
NS = 32
NB = 8
ZL = BOX // NS
YL = BOX // NB
XL = BOX // NB
CH = 3
ZC = ZL // CH
PIECE = 24
CHIPS = NS // 2
LANES = 640
F32 = jnp.float32
BF16 = jnp.bfloat16
VMEM = pl.BlockSpec(memory_space=pltpu.VMEM)
SMEM = pl.BlockSpec(memory_space=pltpu.SMEM)
LIMIT = 58 * 1024 * 1024


def dft_tables():
    index = np.arange(BOX, dtype=np.int64)
    phases = (index[:, None] * index[None, :] % BOX).astype(np.float64)
    angles = phases * (2.0 * math.pi / BOX)
    factor = 1.0 / math.sqrt(BOX)
    return np.cos(angles) * factor, np.sin(angles) * factor


def pass_tables():
    cos, sin = dft_tables()
    x_tab = np.concatenate([cos, -sin], axis=0).T
    full = np.stack([np.stack([cos, sin], 1), np.stack([-sin, cos], 1)], 0)
    y_tab = full.reshape(2, NB, YL, 2, NS, ZL).transpose(4, 3, 5, 1, 0, 2).reshape(2 * BOX, 2 * BOX)
    z_tab = full.reshape(2, NS, ZL, 2, BOX).transpose(2, 0, 1, 3, 4).reshape(2 * BOX, 2 * BOX)
    return tuple(jnp.asarray(t.astype(np.float32), F32).astype(BF16) for t in (x_tab, y_tab, z_tab))


def sums_kernel(orient_ref, defocus_ref, image_ref, ctf_ref, sum_ref, count_ref):
    block = pl.program_id(0)
    count = image_ref.shape[0]
    row = lax.broadcasted_iota(jnp.int32, count_ref.shape, 0)
    lane = lax.broadcasted_iota(jnp.int32, count_ref.shape, 1)

    @pl.when(block == 0)
    def _():
        sum_ref[...] = jnp.zeros_like(sum_ref)
        count_ref[...] = jnp.zeros_like(count_ref)

    def step(i, total):
        p = block * count + i
        orient, defocus = orient_ref[p], defocus_ref[p]
        ctf = ctf_ref[defocus].astype(F32)
        for h in range(2):
            cols = slice(h * BOX, (h + 1) * BOX)
            sum_ref[orient, :, cols] += ctf * image_ref[i, :, cols].astype(F32)
        return total + jnp.where((row == orient) & (lane == defocus), 1.0, 0.0)

    count_ref[...] = lax.fori_loop(0, count, step, count_ref[...])


def local_sums(orient_ids, defocus_ids, images, ctf_tables):
    block = 8
    whole = lambda *shape: pl.BlockSpec(shape, lambda i: (0,) * len(shape))
    return pl.pallas_call(
        sums_kernel,
        grid=(images.shape[0] // block,),
        out_shape=(
            jax.ShapeDtypeStruct((ORI, YL, 2 * BOX), F32),
            jax.ShapeDtypeStruct((8, 128), F32),
        ),
        in_specs=[
            SMEM,
            SMEM,
            pl.BlockSpec((block, YL, 2 * BOX), lambda i: (i, 0, 0)),
            whole(DEF, YL, BOX),
        ],
        out_specs=(whole(ORI, YL, 2 * BOX), whole(8, 128)),
        compiler_params=pltpu.CompilerParams(vmem_limit_bytes=LIMIT),
        name="local_sums",
    )(orient_ids, defocus_ids, images, ctf_tables)


def slab_copy(src, dst, send, recv, to):
    return pltpu.make_async_remote_copy(
        src_ref=src, dst_ref=dst, send_sem=send, recv_sem=recv,
        device_id={"slab": to}, device_id_type=pl.DeviceIdType.MESH,
    )


def batch_copy(src, dst, send, recv, to):
    return pltpu.make_async_remote_copy(
        src_ref=src, dst_ref=dst, send_sem=send, recv_sem=recv,
        device_id={"batch": to}, device_id_type=pl.DeviceIdType.MESH,
    )


def interp_row(tilt):
    column = lax.broadcasted_iota(jnp.int32, (1, BOX), 1)
    position = HALF * 256 + (column - HALF) * tilt
    low = position >> 8
    fraction = (position & 255).astype(F32) * (1.0 / 256.0)
    return low, fraction


OFFSETS = [(2, 2), (3, 2), (2, 3), (1, 2), (2, 1), (0, 2), (2, 0), (3, 1), (1, 3), (3, 3), (1, 1), (0, 3), (0, 1), (3, 0), (1, 0)]
GROUPS = ((0, 2), (2, 3))


def main_kernel(
    sum_ref, count_ref, volume_ref, ctf_ref, tz_ref, tx_ref, xtab_ref, ytab_ref,
    out_ref,
    vol, ctf_buf, x_tab, y_tab, width, depth, proj, numer, power, operand, weight, paired,
    pair_buf, piece_buf, part_buf, total_buf, sums, count_buf, count_pair,
    along_x, pieces, gathered, along_y,
    load, pair_send, pair_recv, part_send, part_recv, gather_send, gather_recv, twin_send, twin_recv,
    count_send, count_recv, halo_send, halo_recv, batch_send, batch_recv, batch_own, slab_send, slab_recv, slab_own,
):
    me = lax.axis_index("slab")
    row_block = lax.axis_index("batch")
    core = lax.rem(me, 2)
    chip = me // 2
    chip_x = lax.rem(chip, 4)
    chip_y = chip // 4
    twin = me + 1 - 2 * core
    below = lax.rem(me + NS - 1, NS)
    above = lax.rem(me + 1, NS)

    loads = [
        pltpu.make_async_copy(volume_ref, vol.at[pl.ds(1, ZL)], load.at[0]),
        pltpu.make_async_copy(ctf_ref, ctf_buf, load.at[1]),
        pltpu.make_async_copy(xtab_ref, x_tab, load.at[2]),
        pltpu.make_async_copy(ytab_ref, y_tab, load.at[3]),
    ]
    for copy in loads:
        copy.start()

    def chip_at(d):
        x, y = OFFSETS[d]
        return 4 * lax.rem(chip_y + y, 4) + lax.rem(chip_x + x, 4)

    def chip_from(d):
        x, y = OFFSETS[d]
        return 4 * lax.rem(chip_y + 4 - y, 4) + lax.rem(chip_x + 4 - x, 4)

    mesh_id = pl.DeviceIdType.MESH
    barrier = pltpu.get_barrier_semaphore()

    def greet(d, _):
        pl.semaphore_signal(barrier, inc=1, device_id={"slab": lax.rem(me + d, NS)}, device_id_type=mesh_id)
        return 0

    lax.fori_loop(1, NS, greet, 0)

    def greet_batch(d, _):
        pl.semaphore_signal(barrier, inc=1, device_id={"batch": lax.rem(row_block + d, NB)}, device_id_type=mesh_id)
        return 0

    lax.fori_loop(1, NB, greet_batch, 0)

    plane = lax.broadcasted_iota(jnp.int32, (16, BOX), 0) + (me * ZL - 1)
    column = lax.broadcasted_iota(jnp.int32, (BOX, BOX), 0)
    for o in range(ORI):
        low, frac = interp_row(tz_ref[o])
        weights = jnp.where(plane == low, 1.0 - frac, 0.0) + jnp.where(plane == low + 1, frac, 0.0)
        depth[o] = jnp.where(plane < BOX, weights, 0.0)
        low, frac = interp_row(tx_ref[o])
        table = jnp.where(column == low, 1.0 - frac, 0.0) + jnp.where(column == low + 1, frac, 0.0)
        width[:, o * BOX : (o + 1) * BOX] = table.astype(BF16)

    pl.semaphore_wait(barrier, NS + NB - 2)

    rows = ORI * YL // 2
    keep = pl.multiple_of(rows * core, rows)
    give = pl.multiple_of(rows * (1 - core), rows)
    pair = slab_copy(sum_ref.at[pl.ds(give, rows)], pair_buf, pair_send, pair_recv, twin)
    pair.start()
    count_twin = slab_copy(count_ref, count_pair, count_send.at[15], count_recv.at[15], twin)
    count_twin.start()
    loads[0].wait()
    halo_up = slab_copy(vol.at[ZL], vol.at[0], halo_send.at[0], halo_recv.at[0], above)
    halo_up.start()
    halo_down = slab_copy(vol.at[1], vol.at[ZL + 1], halo_send.at[1], halo_recv.at[1], below)
    halo_down.start()

    def project(o):
        for h in range(2):
            cols = slice(h * BOX, (h + 1) * BOX)
            seen = jnp.dot(
                vol[:, :, cols].reshape((ZL + 2) * YL, BOX), width[:, o * BOX : (o + 1) * BOX],
                preferred_element_type=F32,
            ).reshape(ZL + 2, YL, BOX)
            total = jnp.zeros((YL, BOX), F32)
            for j in range(ZL + 2):
                total = total + depth[o, j : j + 1, :] * seen[j]
            proj[o, :, cols] = total

    count_twin.wait()
    count_buf[15] = count_ref[...] + count_pair[...]
    counts = [
        slab_copy(count_buf.at[15], count_buf.at[d], count_send.at[d], count_recv.at[d], 2 * chip_at(d) + core)
        for d in range(15)
    ]
    for copy in counts:
        copy.start()
    halo_up.wait()
    halo_down.wait()
    project(0)
    project(1)

    pair.wait()
    for j in range(CHIPS):
        r, c = PIECE * (j // 2), BOX * (j % 2)
        piece_buf[j] = (
            sum_ref[pl.ds(pl.multiple_of(keep + r, 8), PIECE), c : c + BOX] + pair_buf[r : r + PIECE, c : c + BOX]
        )
    parts = [
        slab_copy(piece_buf.at[chip_at(d)], part_buf.at[d], part_send.at[d], part_recv.at[d], 2 * chip_at(d) + core)
        for d in range(15)
    ]
    for copy in parts:
        copy.start()
    for o in range(2, ORI):
        project(o)
    total = piece_buf[chip]
    for d in range(15):
        parts[d].wait()
        total = total + part_buf[d]
    total_buf[...] = total

    def place(ref, which):
        r = pl.multiple_of(keep + PIECE * (which // 2), 8)
        c = pl.multiple_of(BOX * lax.rem(which, 2), 128)
        return ref.at[pl.ds(r, PIECE), pl.ds(c, BOX)]

    gathers = [
        slab_copy(total_buf, place(sums, chip), gather_send.at[d], gather_recv.at[d], 2 * chip_at(d) + core)
        for d in range(15)
    ]
    for copy in gathers:
        copy.start()
    own_r = pl.multiple_of(keep + PIECE * (chip // 2), 8)
    own_c = pl.multiple_of(BOX * lax.rem(chip, 2), 128)
    sums[pl.ds(own_r, PIECE), pl.ds(own_c, BOX)] = total_buf[...]
    twins = [
        slab_copy(place(sums, w), place(sums, w), twin_send.at[d], twin_recv.at[d], twin)
        for d, w in enumerate([chip_from(d) for d in range(15)] + [chip])
    ]
    twins[15].start()

    number = count_buf[15]
    for d in range(15):
        counts[d].wait()
        number = number + count_buf[d]
    loads[1].wait()
    ctf = ctf_buf[...].astype(F32)
    square = ctf * ctf
    for o in range(ORI):
        have = jnp.zeros((YL, BOX), F32)
        for d in range(DEF):
            have = have + number[o : o + 1, d : d + 1] * square[d]
        power[o] = have
        k = slice(o * BOX, (o + 1) * BOX)
        for z in range(ZL):
            operand[z * YL : (z + 1) * YL, k] = (depth[o, z + 1 : z + 2, :] * have).astype(BF16)
    weight[...] = lax.dot_general(
        operand[...], width[...], (((1,), (1,)), ((), ())), preferred_element_type=F32
    ) + TAU

    for d in range(15):
        gathers[d].wait()
        twins[d].start()
    for d in range(16):
        twins[d].wait()
    for o in range(ORI):
        for h in range(2):
            cols = slice(h * BOX, (h + 1) * BOX)
            numer[o, :, cols] = sums[o * YL : (o + 1) * YL, cols] - power[o] * proj[o, :, cols]

    loads[2].wait()

    def batch_piece(c, d):
        to = lax.rem(row_block + d, NB)
        return batch_copy(along_x.at[c, to], pieces.at[c, row_block], batch_send.at[c, d], batch_recv.at[c, d], to)

    def batch_local(c):
        return pltpu.make_async_copy(along_x.at[c, row_block], pieces.at[c, row_block], batch_own.at[c])

    for c in range(CH):
        for o in range(ORI):
            k = slice(o * BOX, (o + 1) * BOX)
            for zi in range(ZC):
                w = depth[o, c * ZC + zi + 1 : c * ZC + zi + 2, :]
                for h in range(2):
                    r = (zi * 2 + h) * YL
                    operand[r : r + YL, k] = (w * numer[o, :, h * BOX : (h + 1) * BOX]).astype(BF16)
        back = lax.dot_general(
            operand[: 2 * ZC * YL, :], width[...], (((1,), (1,)), ((), ())), preferred_element_type=F32
        )
        for zi in range(ZC):
            z = c * ZC + zi
            part = []
            for h in range(2):
                r = (zi * 2 + h) * YL
                old = vol[z + 1, :, h * BOX : (h + 1) * BOX].astype(F32)
                part.append((old + back[r : r + YL] / weight[z * YL : (z + 1) * YL, :]).astype(BF16))
            r = zi * 2 * YL
            paired[r : r + YL, :BOX] = part[0]
            paired[r : r + YL, BOX:] = part[1]
            paired[r + YL : r + 2 * YL, :BOX] = part[1]
            paired[r + YL : r + 2 * YL, BOX:] = -part[0]
        along_x[c] = lax.dot_general(
            x_tab[...], paired[...], (((1,), (1,)), ((), ())), preferred_element_type=F32
        ).astype(BF16).reshape(NB, XL, ZC * 2 * YL)
        for d in (4, 3, 5, 2, 6, 1, 7):
            batch_piece(c, d).start()
        batch_local(c).start()

    loads[3].wait()

    def slab_piece(g, d, e):
        lanes = pl.ds(GROUPS[g][0] * ZC * XL, (384, 256)[g])
        to = 2 * chip_at(d) + (core if e == 0 else 1 - core) if d < 15 else twin
        return slab_copy(
            along_y.at[to, :, lanes], out_ref.at[me, :, lanes], slab_send.at[g, 2 * d + e], slab_recv.at[g, 2 * d + e], to
        )

    def slab_local(g):
        lanes = pl.ds(GROUPS[g][0] * ZC * XL, (384, 256)[g])
        return pltpu.make_async_copy(along_y.at[me, :, lanes], out_ref.at[me, :, lanes], slab_own.at[g])

    targets = [(d, e) for d in range(15) for e in range(2)] + [(15, 0)]
    along_y[:, :, ZL * XL :] = jnp.zeros((NS, 2 * ZL, LANES - ZL * XL), BF16)
    for g, (first, last) in enumerate(GROUPS):
        for c in range(first, last):
            for d in range(1, NB):
                batch_piece(c, d).wait()
            batch_local(c).wait()
            for zi in range(ZC):
                z = c * ZC + zi
                lanes = slice(zi * 2 * YL, (zi + 1) * 2 * YL)
                gathered[z * XL : (z + 1) * XL, :] = jnp.concatenate(
                    [pieces[c, b, :, lanes] for b in range(NB)], axis=1
                )
        low, high = first * ZC * XL, last * ZC * XL
        out = lax.dot_general(
            y_tab[...], gathered[low:high, :], (((1,), (1,)), ((), ())), preferred_element_type=F32
        )
        along_y[:, :, low:high] = out.astype(BF16).reshape(NS, 2 * ZL, high - low)
        for d, e in targets:
            slab_piece(g, d, e).start()
        slab_local(g).start()
    for g in range(len(GROUPS)):
        for d, e in targets:
            slab_piece(g, d, e).wait()
        slab_local(g).wait()


def main(sums, counts, volume, ctf_tables, tilt_z, tilt_x, x_tab, y_tab):
    dma = pltpu.SemaphoreType.DMA
    any_space = pl.BlockSpec(memory_space=pl.ANY)
    half = ORI * YL // 2
    return pl.pallas_call(
        main_kernel,
        out_shape=jax.ShapeDtypeStruct((NS, 2 * ZL, LANES), BF16),
        in_specs=[VMEM, VMEM, any_space, any_space, SMEM, SMEM, any_space, any_space],
        out_specs=VMEM,
        scratch_shapes=[
            pltpu.VMEM((ZL + 2, YL, 2 * BOX), BF16),
            pltpu.VMEM((DEF, YL, BOX), BF16),
            pltpu.VMEM((BOX, 2 * BOX), BF16),
            pltpu.VMEM((2 * BOX, 2 * BOX), BF16),
            pltpu.VMEM((BOX, ORI * BOX), BF16),
            pltpu.VMEM((ORI, 16, BOX), F32),
            pltpu.VMEM((ORI, YL, 2 * BOX), F32),
            pltpu.VMEM((ORI, YL, 2 * BOX), F32),
            pltpu.VMEM((ORI, YL, BOX), F32),
            pltpu.VMEM((ZL * YL, ORI * BOX), BF16),
            pltpu.VMEM((ZL * YL, BOX), F32),
            pltpu.VMEM((ZC * 2 * YL, 2 * BOX), BF16),
            pltpu.VMEM((half, 2 * BOX), F32),
            pltpu.VMEM((CHIPS, PIECE, BOX), F32),
            pltpu.VMEM((CHIPS - 1, PIECE, BOX), F32),
            pltpu.VMEM((PIECE, BOX), F32),
            pltpu.VMEM((ORI * YL, 2 * BOX), F32),
            pltpu.VMEM((CHIPS, 8, 128), F32),
            pltpu.VMEM((8, 128), F32),
            pltpu.VMEM((CH, NB, XL, ZC * 2 * YL), BF16),
            pltpu.VMEM((CH, NB, XL, ZC * 2 * YL), BF16),
            pltpu.VMEM((ZL * XL, 2 * BOX), BF16),
            pltpu.VMEM((NS, 2 * ZL, LANES), BF16),
            dma((4,)), dma(()), dma(()), dma((15,)), dma((15,)), dma((15,)), dma((15,)), dma((16,)), dma((16,)),
            dma((16,)), dma((16,)), dma((2,)), dma((2,)), dma((CH, NB)), dma((CH, NB)), dma((CH,)),
            dma((2, 32)), dma((2, 32)), dma((2,)),
        ],
        compiler_params=pltpu.CompilerParams(vmem_limit_bytes=LIMIT, collective_id=0, has_side_effects=True),
        name="main",
    )(sums, counts, volume, ctf_tables, tilt_z, tilt_x, x_tab, y_tab)


def zpass_kernel(in_ref, ztab_ref, out_ref, wide, gathered):
    for t in range(LANES // 128):
        lanes = slice(t * 128, (t + 1) * 128)
        wide[t] = in_ref[:, :, lanes].astype(F32).reshape(NS * 2 * ZL, 128)
    for z in range(ZL):
        lane = z * XL
        t, off = lane // 128, lane % 128
        for h in range(2):
            blocks = []
            for y in range(ZL):
                rows = pl.ds(h * ZL + y, NS, 2 * ZL)
                if off + XL <= 128:
                    blocks.append(wide[t, rows, :][:, off : off + XL])
                else:
                    both = jnp.concatenate([wide[t, rows, :], wide[t + 1, rows, :]], axis=1)
                    blocks.append(both[:, off : off + XL])
            r = (z * 2 + h) * NS
            gathered[r : r + NS, :] = jnp.concatenate(blocks, axis=1).astype(BF16)
    out = lax.dot_general(gathered[...], ztab_ref[...], (((0,), (0,)), ((), ())), preferred_element_type=F32)
    out_ref[0] = out[:, :BOX]
    out_ref[1] = out[:, BOX:]


def zpass(x, z_tab):
    return pl.pallas_call(
        zpass_kernel,
        out_shape=jax.ShapeDtypeStruct((2, ZL * XL, BOX), F32),
        in_specs=[VMEM, VMEM],
        out_specs=VMEM,
        scratch_shapes=[
            pltpu.VMEM((LANES // 128, NS * 2 * ZL, 128), F32),
            pltpu.VMEM((2 * BOX, ZL * XL), BF16),
        ],
        compiler_params=pltpu.CompilerParams(vmem_limit_bytes=LIMIT),
        name="zpass",
    )(x, z_tab)


def local(volume, images, orient_ids, defocus_ids, ctf_tables, tilt_z, tilt_x):
    x_tab, y_tab, z_tab = pass_tables()
    sums, counts = local_sums(orient_ids, defocus_ids, images, ctf_tables)
    pieces = main(
        sums.reshape(ORI * YL, 2 * BOX), counts, volume, ctf_tables, tilt_z, tilt_x, x_tab, y_tab
    )
    return zpass(pieces, z_tab).reshape(2, ZL, XL, BOX)


def solution(mesh):
    in_specs = (
        P("slab", "batch", None),
        P("slab", "batch", None),
        P("slab"),
        P("slab"),
        P(None, "batch", None),
        P(),
        P(),
    )
    out_specs = P(None, "slab", "batch", None)
    return jax.shard_map(local, mesh=mesh, in_specs=in_specs, out_specs=out_specs, check_vma=False)
```

```python
import functools
import math

import jax
import jax.numpy as jnp
import numpy as np
from jax import lax
from jax.experimental import pallas as pl
from jax.experimental.pallas import tpu as pltpu
from jax.sharding import PartitionSpec as P

TAU = 1.0
BOX = 384
HALF = 192
ORI = 8
DEF = 8
NS = 32
NB = 8
ZL = BOX // NS
YL = BOX // NB
XL = BOX // NB
CH = 3
ZC = ZL // CH
PARTS = ((0, 16), (16, 32))
CHIPS = NS // 2
LANES = 640
F32 = jnp.float32
BF16 = jnp.bfloat16
VMEM = pl.BlockSpec(memory_space=pltpu.VMEM)
SMEM = pl.BlockSpec(memory_space=pltpu.SMEM)
LIMIT = 58 * 1024 * 1024


def dft_tables():
    index = np.arange(BOX, dtype=np.int64)
    phases = (index[:, None] * index[None, :] % BOX).astype(np.float64)
    angles = phases * (2.0 * math.pi / BOX)
    factor = 1.0 / math.sqrt(BOX)
    return np.cos(angles) * factor, np.sin(angles) * factor


def pass_tables():
    cos, sin = dft_tables()
    x_tab = np.concatenate([cos, -sin], axis=0).T
    full = np.stack([np.stack([cos, sin], 1), np.stack([-sin, cos], 1)], 0)
    split = full.reshape(2, NB, YL, 2, NS, ZL).transpose(4, 3, 5, 1, 0, 2)
    y_tab = np.concatenate(
        [split[..., y : y + n].reshape(2 * BOX, NB * 2 * n) for y, n in PARTS], axis=1
    )
    z_tab = full.reshape(2, NS, ZL, 2, BOX).transpose(2, 0, 1, 3, 4).reshape(2 * BOX, 2 * BOX)
    return tuple(jnp.asarray(t.astype(np.float32), F32).astype(BF16) for t in (x_tab, y_tab, z_tab))


def slab_copy(src, dst, send, recv, to):
    return pltpu.make_async_remote_copy(
        src_ref=src, dst_ref=dst, send_sem=send, recv_sem=recv,
        device_id={"slab": to}, device_id_type=pl.DeviceIdType.MESH,
    )


def batch_copy(src, dst, send, recv, to):
    return pltpu.make_async_remote_copy(
        src_ref=src, dst_ref=dst, send_sem=send, recv_sem=recv,
        device_id={"batch": to}, device_id_type=pl.DeviceIdType.MESH,
    )


def interp_row(tilt):
    column = lax.broadcasted_iota(jnp.int32, (1, BOX), 1)
    position = HALF * 256 + (column - HALF) * tilt
    low = position >> 8
    fraction = (position & 255).astype(F32) * (1.0 / 256.0)
    return low, fraction


OFFSETS = [(2, 2), (3, 2), (2, 3), (1, 2), (2, 1), (0, 2), (2, 0), (3, 1), (1, 3), (3, 3), (1, 1), (0, 3), (0, 1), (3, 0), (1, 0)]
GROUPS = ((0, 2), (2, 3))


def main_kernel(
    orient_ref, defocus_ref, tz_ref, tx_ref, image_ref, volume_ref, ctf_ref, xtab_ref, ytab_ref,
    out_ref,
    image0, image1, vol, ctf_buf, x_tab, y_tab, width, depth, proj, power, operand, weight, paired,
    local0, local1, pair0, pair1, piece0, piece1, part0, part1, total0, total1, sums0, sums1,
    count_buf, count_pair, count_own,
    along0, along1, pieces0, pieces1, gathered, along_y,
    load, pair_send, pair_recv, part_send, part_recv, gather_send, gather_recv, twin_send, twin_recv,
    count_send, count_recv, halo_send, halo_recv, batch_send, batch_recv, batch_own, slab_send, slab_recv, slab_own,
):
    me = lax.axis_index("slab")
    row_block = lax.axis_index("batch")
    core = lax.rem(me, 2)
    chip = me // 2
    chip_x = lax.rem(chip, 4)
    chip_y = chip // 4
    twin = me + 1 - 2 * core
    below = lax.rem(me + NS - 1, NS)
    above = lax.rem(me + 1, NS)
    images, locals_, pairs = (image0, image1), (local0, local1), (pair0, pair1)
    pieces_, parts_, totals, sums = (piece0, piece1), (part0, part1), (total0, total1), (sums0, sums1)

    loads = [
        pltpu.make_async_copy(src, dst, load.at[i])
        for i, (src, dst) in enumerate([
            (ctf_ref, ctf_buf),
            (image_ref.at[:, pl.ds(PARTS[0][0], PARTS[0][1])], image0),
            (image_ref.at[:, pl.ds(PARTS[1][0], PARTS[1][1])], image1),
            (volume_ref, vol.at[pl.ds(1, ZL)]),
            (xtab_ref, x_tab),
            (ytab_ref, y_tab),
        ])
    ]
    for copy in loads:
        copy.start()

    def chip_at(d):
        x, y = OFFSETS[d]
        return 4 * lax.rem(chip_y + y, 4) + lax.rem(chip_x + x, 4)

    def chip_from(d):
        x, y = OFFSETS[d]
        return 4 * lax.rem(chip_y + 4 - y, 4) + lax.rem(chip_x + 4 - x, 4)

    mesh_id = pl.DeviceIdType.MESH
    barrier = pltpu.get_barrier_semaphore()

    def greet(d, _):
        pl.semaphore_signal(barrier, inc=1, device_id={"slab": lax.rem(me + d, NS)}, device_id_type=mesh_id)
        return 0

    lax.fori_loop(1, NS, greet, 0)

    def greet_batch(d, _):
        pl.semaphore_signal(barrier, inc=1, device_id={"batch": lax.rem(row_block + d, NB)}, device_id_type=mesh_id)
        return 0

    lax.fori_loop(1, NB, greet_batch, 0)

    plane = lax.broadcasted_iota(jnp.int32, (16, BOX), 0) + (me * ZL - 1)
    column = lax.broadcasted_iota(jnp.int32, (BOX, BOX), 0)
    for o in range(ORI):
        low, frac = interp_row(tz_ref[o])
        weights = jnp.where(plane == low, 1.0 - frac, 0.0) + jnp.where(plane == low + 1, frac, 0.0)
        depth[o] = jnp.where(plane < BOX, weights, 0.0)
        low, frac = interp_row(tx_ref[o])
        table = jnp.where(column == low, 1.0 - frac, 0.0) + jnp.where(column == low + 1, frac, 0.0)
        width[:, o * BOX : (o + 1) * BOX] = table.astype(BF16)

    def local_sums(part):
        for r in range(0, PARTS[part][1], 16):
            for t in range(0, BOX, 128):
                def step(p, totals_):
                    orient, defocus = orient_ref[p], defocus_ref[p]
                    ctf = ctf_buf[defocus, PARTS[part][0] + r : PARTS[part][0] + r + 16, t : t + 128].astype(F32)
                    terms = [
                        ctf * images[part][p, r : r + 16, h * BOX + t : h * BOX + t + 128].astype(F32) for h in range(2)
                    ]
                    hot = [jnp.where(orient == o, 1.0, 0.0) for o in range(ORI)]
                    return tuple(totals_[2 * o + h] + hot[o] * terms[h] for o in range(ORI) for h in range(2))

                have = lax.fori_loop(0, 32, step, tuple(jnp.zeros((16, 128), F32) for _ in range(2 * ORI)))
                for o in range(ORI):
                    for h in range(2):
                        row = o * PARTS[part][1] + r
                        locals_[part][row : row + 16, h * BOX + t : h * BOX + t + 128] = have[2 * o + h]

    loads[0].wait()
    loads[1].wait()
    local_sums(0)

    pl.semaphore_wait(barrier, NS + NB - 2)

    def half(part):
        rows = ORI * PARTS[part][1] // 2
        return rows, pl.multiple_of(rows * core, rows), pl.multiple_of(rows * (1 - core), rows)

    def pair_copy(part):
        rows, _, give = half(part)
        return slab_copy(
            locals_[part].at[pl.ds(give, rows)], pairs[part], pair_send.at[part], pair_recv.at[part], twin
        )

    pair_copy(0).start()
    row = lax.broadcasted_iota(jnp.int32, (8, 128), 0)
    lane = lax.broadcasted_iota(jnp.int32, (8, 128), 1)

    def count_step(p, have):
        return have + jnp.where((row == orient_ref[p]) & (lane == defocus_ref[p]), 1.0, 0.0)

    count_own[...] = lax.fori_loop(0, 32, count_step, jnp.zeros((8, 128), F32))
    count_twin = slab_copy(count_own, count_pair, count_send.at[15], count_recv.at[15], twin)
    count_twin.start()
    loads[3].wait()
    halo_up = slab_copy(vol.at[ZL], vol.at[0], halo_send.at[0], halo_recv.at[0], above)
    halo_up.start()
    halo_down = slab_copy(vol.at[1], vol.at[ZL + 1], halo_send.at[1], halo_recv.at[1], below)
    halo_down.start()
    loads[2].wait()
    local_sums(1)
    pair_copy(1).start()

    def part_copies(part):
        return [
            slab_copy(
                pieces_[part].at[chip_at(d)], parts_[part].at[d],
                part_send.at[part, d], part_recv.at[part, d], 2 * chip_at(d) + core,
            )
            for d in range(15)
        ]

    def spread_pieces(part):
        _, keep, _ = half(part)
        n = PARTS[part][1] // 2
        pair_copy(part).wait()
        for j in range(CHIPS):
            r, c = n * (j // 2), BOX * (j % 2)
            pieces_[part][j] = (
                locals_[part][pl.ds(pl.multiple_of(keep + r, 8), n), c : c + BOX]
                + pairs[part][r : r + n, c : c + BOX]
            )
        for copy in part_copies(part):
            copy.start()

    def place(part, which):
        _, keep, _ = half(part)
        n = PARTS[part][1] // 2
        r = pl.multiple_of(keep + n * (which // 2), 8)
        c = pl.multiple_of(BOX * lax.rem(which, 2), 128)
        return pl.ds(r, n), pl.ds(c, BOX)

    def gather_copies(part):
        return [
            slab_copy(
                totals[part], sums[part].at[place(part, chip)],
                gather_send.at[part, d], gather_recv.at[part, d], 2 * chip_at(d) + core,
            )
            for d in range(15)
        ]

    def twin_copies(part):
        return [
            slab_copy(
                sums[part].at[place(part, w)], sums[part].at[place(part, w)],
                twin_send.at[part, d], twin_recv.at[part, d], twin,
            )
            for d, w in enumerate([chip_from(d) for d in range(15)] + [chip])
        ]

    def add_pieces(part):
        total = pieces_[part][chip]
        for d, copy in enumerate(part_copies(part)):
            copy.wait()
            total = total + parts_[part][d]
        totals[part][...] = total
        for copy in gather_copies(part):
            copy.start()
        sums[part][place(part, chip)] = total
        twin_copies(part)[15].start()

    def forward_pieces(part):
        for gather, forward in zip(gather_copies(part), twin_copies(part)[:15]):
            gather.wait()
            forward.start()

    def take_sums(part):
        for copy in twin_copies(part):
            copy.wait()

    def project(part, o):
        y, n = PARTS[part]
        for h in range(2):
            cols = slice(h * BOX, (h + 1) * BOX)
            seen = jnp.dot(
                vol[:, y : y + n, cols].reshape((ZL + 2) * n, BOX), width[:, o * BOX : (o + 1) * BOX],
                preferred_element_type=F32,
            ).reshape(ZL + 2, n, BOX)
            total = jnp.zeros((n, BOX), F32)
            for j in range(ZL + 2):
                total = total + depth[o, j : j + 1, :] * seen[j]
            proj[o, y : y + n, cols] = total

    spread_pieces(0)
    count_twin.wait()
    count_buf[15] = count_own[...] + count_pair[...]
    counts = [
        slab_copy(count_buf.at[15], count_buf.at[d], count_send.at[d], count_recv.at[d], 2 * chip_at(d) + core)
        for d in range(15)
    ]
    for copy in counts:
        copy.start()
    halo_up.wait()
    halo_down.wait()
    for o in range(4):
        project(0, o)
    spread_pieces(1)
    for o in range(4, ORI):
        project(0, o)
    add_pieces(0)

    number = count_buf[15]
    for d in range(15):
        counts[d].wait()
        number = number + count_buf[d]
    ctf_all = ctf_buf[...].astype(F32)
    square = ctf_all * ctf_all
    for o in range(ORI):
        have = jnp.zeros((YL, BOX), F32)
        for d in range(DEF):
            have = have + number[o : o + 1, d : d + 1] * square[d]
        power[o] = have
        k = slice(o * BOX, (o + 1) * BOX)
        for z in range(ZL):
            operand[z * YL : (z + 1) * YL, k] = (depth[o, z + 1 : z + 2, :] * have).astype(BF16)
    weight[...] = lax.dot_general(
        operand[...], width[...], (((1,), (1,)), ((), ())), preferred_element_type=F32
    ) + TAU
    add_pieces(1)
    forward_pieces(0)
    for o in range(2):
        project(1, o)
    take_sums(0)
    loads[4].wait()

    def update(part, first, last):
        y, n = PARTS[part]
        count = last - first
        for o in range(ORI):
            k = slice(o * BOX, (o + 1) * BOX)
            for h in range(2):
                cols = slice(h * BOX, (h + 1) * BOX)
                numer = sums[part][o * n : (o + 1) * n, cols] - power[o, y : y + n, :] * proj[o, y : y + n, cols]
                for zi in range(count):
                    r = (zi * 2 + h) * n
                    w = depth[o, first + zi + 1 : first + zi + 2, :]
                    operand[r : r + n, k] = (w * numer).astype(BF16)
        m = count * 2 * n
        back = lax.dot_general(
            operand[:m, :], width[...], (((1,), (1,)), ((), ())), preferred_element_type=F32
        )
        for zi in range(count):
            z = first + zi
            fresh = []
            for h in range(2):
                r = (zi * 2 + h) * n
                old = vol[z + 1, y : y + n, h * BOX : (h + 1) * BOX].astype(F32)
                fresh.append((old + back[r : r + n] / weight[z * YL + y : z * YL + y + n, :]).astype(BF16))
            r = zi * 2 * n
            paired[r : r + n, :BOX] = fresh[0]
            paired[r : r + n, BOX:] = fresh[1]
            paired[r + n : r + 2 * n, :BOX] = fresh[1]
            paired[r + n : r + 2 * n, BOX:] = -fresh[0]
        return lax.dot_general(
            x_tab[...], paired[:m, :], (((1,), (1,)), ((), ())), preferred_element_type=F32
        ).astype(BF16).reshape(NB, XL, m)

    def batch_piece(c, d):
        to = lax.rem(row_block + d, NB)
        src = along0.at[to] if c == 0 else along1.at[c - 1, to]
        dst = pieces0.at[row_block] if c == 0 else pieces1.at[c - 1, row_block]
        return batch_copy(src, dst, batch_send.at[c, d], batch_recv.at[c, d], to)

    def batch_local(c):
        src = along0.at[row_block] if c == 0 else along1.at[c - 1, row_block]
        dst = pieces0.at[row_block] if c == 0 else pieces1.at[c - 1, row_block]
        return pltpu.make_async_copy(src, dst, batch_own.at[c])

    def batch_go(c):
        for d in (4, 3, 5, 2, 6, 1, 7):
            batch_piece(c, d).start()
        batch_local(c).start()

    def batch_done(c):
        for d in range(1, NB):
            batch_piece(c, d).wait()
        batch_local(c).wait()

    along0[...] = update(0, 0, ZL)
    batch_go(0)
    forward_pieces(1)
    for o in range(2, ORI):
        project(1, o)
    take_sums(1)
    for c in range(CH):
        along1[c] = update(1, c * ZC, (c + 1) * ZC)
        batch_go(c + 1)

    loads[5].wait()

    def slab_piece(g, d, e):
        lanes = pl.ds(GROUPS[g][0] * ZC * XL, (384, 256)[g])
        to = 2 * chip_at(d) + (core if e == 0 else 1 - core) if d < 15 else twin
        return slab_copy(
            along_y.at[to, :, lanes], out_ref.at[me, :, lanes], slab_send.at[g, 2 * d + e], slab_recv.at[g, 2 * d + e], to
        )

    def slab_local(g):
        lanes = pl.ds(GROUPS[g][0] * ZC * XL, (384, 256)[g])
        return pltpu.make_async_copy(along_y.at[me, :, lanes], out_ref.at[me, :, lanes], slab_own.at[g])

    targets = [(d, e) for d in range(15) for e in range(2)] + [(15, 0)]
    along_y[:, :, ZL * XL :] = jnp.zeros((NS, 2 * ZL, LANES - ZL * XL), BF16)
    wide0, wide1 = (2 * n for _, n in PARTS)
    batch_done(0)
    for z in range(ZL):
        gathered[z * XL : (z + 1) * XL, : NB * wide0] = jnp.concatenate(
            [pieces0[b, :, z * wide0 : (z + 1) * wide0] for b in range(NB)], axis=1
        )
    for g, (first, last) in enumerate(GROUPS):
        for c in range(first, last):
            batch_done(c + 1)
            for zi in range(ZC):
                z = c * ZC + zi
                gathered[z * XL : (z + 1) * XL, NB * wide0 :] = jnp.concatenate(
                    [pieces1[c, b, :, zi * wide1 : (zi + 1) * wide1] for b in range(NB)], axis=1
                )
        low, high = first * ZC * XL, last * ZC * XL
        out = lax.dot_general(
            y_tab[...], gathered[low:high, :], (((1,), (1,)), ((), ())), preferred_element_type=F32
        )
        along_y[:, :, low:high] = out.astype(BF16).reshape(NS, 2 * ZL, high - low)
        for d, e in targets:
            slab_piece(g, d, e).start()
        slab_local(g).start()
    for g in range(len(GROUPS)):
        for d, e in targets:
            slab_piece(g, d, e).wait()
        slab_local(g).wait()


def main(orient_ids, defocus_ids, tilt_z, tilt_x, images, volume, ctf_tables, x_tab, y_tab):
    dma = pltpu.SemaphoreType.DMA
    any_space = pl.BlockSpec(memory_space=pl.ANY)
    two = lambda shape, dtype: [pltpu.VMEM(shape(n), dtype) for _, n in PARTS]
    return pl.pallas_call(
        main_kernel,
        out_shape=jax.ShapeDtypeStruct((NS, 2 * ZL, LANES), BF16),
        in_specs=[SMEM] * 4 + [any_space] * 5,
        out_specs=VMEM,
        scratch_shapes=[
            *two(lambda n: (32, n, 2 * BOX), BF16),
            pltpu.VMEM((ZL + 2, YL, 2 * BOX), BF16),
            pltpu.VMEM((DEF, YL, BOX), BF16),
            pltpu.VMEM((BOX, 2 * BOX), BF16),
            pltpu.VMEM((2 * BOX, 2 * BOX), BF16),
            pltpu.VMEM((BOX, ORI * BOX), BF16),
            pltpu.VMEM((ORI, 16, BOX), F32),
            pltpu.VMEM((ORI, YL, 2 * BOX), F32),
            pltpu.VMEM((ORI, YL, BOX), F32),
            pltpu.VMEM((ZL * YL, ORI * BOX), BF16),
            pltpu.VMEM((ZL * YL, BOX), F32),
            pltpu.VMEM((BOX, 2 * BOX), BF16),
            *two(lambda n: (ORI * n, 2 * BOX), F32),
            *two(lambda n: (ORI * n // 2, 2 * BOX), F32),
            *two(lambda n: (CHIPS, n // 2, BOX), F32),
            *two(lambda n: (CHIPS - 1, n // 2, BOX), F32),
            *two(lambda n: (n // 2, BOX), F32),
            *two(lambda n: (ORI * n, 2 * BOX), F32),
            pltpu.VMEM((CHIPS, 8, 128), F32),
            pltpu.VMEM((8, 128), F32),
            pltpu.VMEM((8, 128), F32),
            pltpu.VMEM((NB, XL, ZL * 2 * PARTS[0][1]), BF16),
            pltpu.VMEM((CH, NB, XL, ZC * 2 * PARTS[1][1]), BF16),
            pltpu.VMEM((NB, XL, ZL * 2 * PARTS[0][1]), BF16),
            pltpu.VMEM((CH, NB, XL, ZC * 2 * PARTS[1][1]), BF16),
            pltpu.VMEM((ZL * XL, 2 * BOX), BF16),
            pltpu.VMEM((NS, 2 * ZL, LANES), BF16),
            dma((6,)), dma((2,)), dma((2,)), dma((2, 15)), dma((2, 15)), dma((2, 15)), dma((2, 15)),
            dma((2, 16)), dma((2, 16)), dma((16,)), dma((16,)), dma((2,)), dma((2,)),
            dma((CH + 1, NB)), dma((CH + 1, NB)), dma((CH + 1,)), dma((2, 32)), dma((2, 32)), dma((2,)),
        ],
        compiler_params=pltpu.CompilerParams(vmem_limit_bytes=LIMIT, collective_id=0, has_side_effects=True),
        name="main",
    )(orient_ids, defocus_ids, tilt_z, tilt_x, images, volume, ctf_tables, x_tab, y_tab)


def zpass_kernel(in_ref, ztab_ref, out_ref, wide, gathered):
    for t in range(LANES // 128):
        lanes = slice(t * 128, (t + 1) * 128)
        wide[t] = in_ref[:, :, lanes].astype(F32).reshape(NS * 2 * ZL, 128)
    for z in range(ZL):
        lane = z * XL
        t, off = lane // 128, lane % 128
        for h in range(2):
            blocks = []
            for y in range(ZL):
                rows = pl.ds(h * ZL + y, NS, 2 * ZL)
                if off + XL <= 128:
                    blocks.append(wide[t, rows, :][:, off : off + XL])
                else:
                    both = jnp.concatenate([wide[t, rows, :], wide[t + 1, rows, :]], axis=1)
                    blocks.append(both[:, off : off + XL])
            r = (z * 2 + h) * NS
            gathered[r : r + NS, :] = jnp.concatenate(blocks, axis=1).astype(BF16)
    out = lax.dot_general(gathered[...], ztab_ref[...], (((0,), (0,)), ((), ())), preferred_element_type=F32)
    out_ref[0] = out[:, :BOX]
    out_ref[1] = out[:, BOX:]


def zpass(x, z_tab):
    return pl.pallas_call(
        zpass_kernel,
        out_shape=jax.ShapeDtypeStruct((2, ZL * XL, BOX), F32),
        in_specs=[VMEM, VMEM],
        out_specs=VMEM,
        scratch_shapes=[
            pltpu.VMEM((LANES // 128, NS * 2 * ZL, 128), F32),
            pltpu.VMEM((2 * BOX, ZL * XL), BF16),
        ],
        compiler_params=pltpu.CompilerParams(vmem_limit_bytes=LIMIT),
        name="zpass",
    )(x, z_tab)


def local(volume, images, orient_ids, defocus_ids, ctf_tables, tilt_z, tilt_x):
    x_tab, y_tab, z_tab = pass_tables()
    pieces = main(orient_ids, defocus_ids, tilt_z, tilt_x, images, volume, ctf_tables, x_tab, y_tab)
    return zpass(pieces, z_tab).reshape(2, ZL, XL, BOX)


def solution(mesh):
    in_specs = (
        P("slab", "batch", None),
        P("slab", "batch", None),
        P("slab"),
        P("slab"),
        P(None, "batch", None),
        P(),
        P(),
    )
    out_specs = P(None, "slab", "batch", None)
    return jax.shard_map(local, mesh=mesh, in_specs=in_specs, out_specs=out_specs, check_vma=False)
```

```python
import functools
import math

import jax
import jax.numpy as jnp
import numpy as np
from jax import lax
from jax.experimental import pallas as pl
from jax.experimental.pallas import tpu as pltpu
from jax.sharding import PartitionSpec as P

TAU = 1.0
BOX = 384
HALF = 192
ORI = 8
DEF = 8
NS = 32
NB = 8
ZL = BOX // NS
YL = BOX // NB
XL = BOX // NB
CH = 3
ZC = ZL // CH
PARTS = ((0, 16), (16, 32))
CHIPS = NS // 2
LANES = 640
F32 = jnp.float32
BF16 = jnp.bfloat16
VMEM = pl.BlockSpec(memory_space=pltpu.VMEM)
SMEM = pl.BlockSpec(memory_space=pltpu.SMEM)
LIMIT = 58 * 1024 * 1024


def dft_tables():
    index = np.arange(BOX, dtype=np.int64)
    phases = (index[:, None] * index[None, :] % BOX).astype(np.float64)
    angles = phases * (2.0 * math.pi / BOX)
    factor = 1.0 / math.sqrt(BOX)
    return np.cos(angles) * factor, np.sin(angles) * factor


def pass_tables():
    cos, sin = dft_tables()
    x_tab = np.concatenate([cos, -sin], axis=0).T
    full = np.stack([np.stack([cos, sin], 1), np.stack([-sin, cos], 1)], 0)
    split = full.reshape(2, NB, YL, 2, NS, ZL).transpose(4, 3, 5, 1, 0, 2)
    y_tab = np.concatenate(
        [split[..., y : y + n].reshape(2 * BOX, NB * 2 * n) for y, n in PARTS], axis=1
    )
    z_tab = full.reshape(2, NS, ZL, 2, BOX).transpose(2, 0, 1, 3, 4).reshape(2 * BOX, 2 * BOX)
    return tuple(jnp.asarray(t.astype(np.float32), F32).astype(BF16) for t in (x_tab, y_tab, z_tab))


def slab_copy(src, dst, send, recv, to):
    return pltpu.make_async_remote_copy(
        src_ref=src, dst_ref=dst, send_sem=send, recv_sem=recv,
        device_id={"slab": to}, device_id_type=pl.DeviceIdType.MESH,
    )


def batch_copy(src, dst, send, recv, to):
    return pltpu.make_async_remote_copy(
        src_ref=src, dst_ref=dst, send_sem=send, recv_sem=recv,
        device_id={"batch": to}, device_id_type=pl.DeviceIdType.MESH,
    )


def interp_row(tilt):
    column = lax.broadcasted_iota(jnp.int32, (1, BOX), 1)
    position = HALF * 256 + (column - HALF) * tilt
    low = position >> 8
    fraction = (position & 255).astype(F32) * (1.0 / 256.0)
    return low, fraction


OFFSETS = [(2, 2), (3, 2), (2, 3), (1, 2), (2, 1), (0, 2), (2, 0), (3, 1), (1, 3), (3, 3), (1, 1), (0, 3), (0, 1), (3, 0), (1, 0)]
GROUPS = ((0, 2), (2, 3))


def main_kernel(
    orient_ref, defocus_ref, tz_ref, tx_ref, image_ref, volume_ref, ctf_ref, xtab_ref, ytab_ref,
    out_ref,
    image0, image1, vol, ctf_buf, x_tab, y_tab, width, depth, proj, power, operand, weight, paired,
    local0, local1, pair0, pair1, piece0, piece1, part0, part1, total0, total1, sums0, sums1,
    count_buf, count_pair, count_own,
    along0, along1, pieces0, pieces1, gathered, along_y, landed, wide, turned,
    load, pair_send, pair_recv, part_send, part_recv, gather_send, gather_recv, twin_send, twin_recv,
    count_send, count_recv, halo_send, halo_recv, batch_send, batch_recv, batch_own, slab_send, slab_recv, slab_own, store,
):
    me = lax.axis_index("slab")
    row_block = lax.axis_index("batch")
    core = lax.rem(me, 2)
    chip = me // 2
    chip_x = lax.rem(chip, 4)
    chip_y = chip // 4
    twin = me + 1 - 2 * core
    below = lax.rem(me + NS - 1, NS)
    above = lax.rem(me + 1, NS)
    images, locals_, pairs = (image0, image1), (local0, local1), (pair0, pair1)
    pieces_, parts_, totals, sums = (piece0, piece1), (part0, part1), (total0, total1), (sums0, sums1)

    def chip_at(d):
        x, y = OFFSETS[d]
        return 4 * lax.rem(chip_y + y, 4) + lax.rem(chip_x + x, 4)

    def chip_from(d):
        x, y = OFFSETS[d]
        return 4 * lax.rem(chip_y + 4 - y, 4) + lax.rem(chip_x + 4 - x, 4)

    mesh_id = pl.DeviceIdType.MESH
    barrier = pltpu.get_barrier_semaphore()

    def greet(d, _):
        pl.semaphore_signal(barrier, inc=1, device_id={"slab": lax.rem(me + d, NS)}, device_id_type=mesh_id)
        return 0

    lax.fori_loop(1, NS, greet, 0)

    def greet_batch(d, _):
        pl.semaphore_signal(barrier, inc=1, device_id={"batch": lax.rem(row_block + d, NB)}, device_id_type=mesh_id)
        return 0

    lax.fori_loop(1, NB, greet_batch, 0)

    loads = [
        pltpu.make_async_copy(src, dst, load.at[i])
        for i, (src, dst) in enumerate([
            (ctf_ref, ctf_buf),
            (image_ref.at[:, pl.ds(PARTS[0][0], PARTS[0][1])], image0),
            (image_ref.at[:, pl.ds(PARTS[1][0], PARTS[1][1])], image1),
            (volume_ref, vol.at[pl.ds(1, ZL)]),
            (xtab_ref, x_tab),
            (ytab_ref, y_tab),
        ])
    ]
    for copy in loads:
        copy.start()

    def local_sums(part):
        for r in range(0, PARTS[part][1], 16):
            for t in range(0, BOX, 128):
                def step(p, totals_):
                    orient, defocus = orient_ref[p], defocus_ref[p]
                    ctf = ctf_buf[defocus, PARTS[part][0] + r : PARTS[part][0] + r + 16, t : t + 128].astype(F32)
                    terms = [
                        ctf * images[part][p, r : r + 16, h * BOX + t : h * BOX + t + 128].astype(F32) for h in range(2)
                    ]
                    hot = [jnp.where(orient == o, 1.0, 0.0) for o in range(ORI)]
                    return tuple(totals_[2 * o + h] + hot[o] * terms[h] for o in range(ORI) for h in range(2))

                have = lax.fori_loop(0, 32, step, tuple(jnp.zeros((16, 128), F32) for _ in range(2 * ORI)), unroll=4)
                for o in range(ORI):
                    for h in range(2):
                        row = o * PARTS[part][1] + r
                        locals_[part][row : row + 16, h * BOX + t : h * BOX + t + 128] = have[2 * o + h]

    loads[0].wait()
    loads[1].wait()
    local_sums(0)
    row = lax.broadcasted_iota(jnp.int32, (8, 128), 0)
    lane = lax.broadcasted_iota(jnp.int32, (8, 128), 1)

    def count_step(p, have):
        return have + jnp.where((row == orient_ref[p]) & (lane == defocus_ref[p]), 1.0, 0.0)

    count_own[...] = lax.fori_loop(0, 32, count_step, jnp.zeros((8, 128), F32), unroll=4)
    loads[3].wait()

    pl.semaphore_wait(barrier, NS + NB - 2)

    def half(part):
        rows = ORI * PARTS[part][1] // 2
        return rows, pl.multiple_of(rows * core, rows), pl.multiple_of(rows * (1 - core), rows)

    def pair_copy(part):
        rows, _, give = half(part)
        return slab_copy(
            locals_[part].at[pl.ds(give, rows)], pairs[part], pair_send.at[part], pair_recv.at[part], twin
        )

    pair_copy(0).start()
    count_twin = slab_copy(count_own, count_pair, count_send.at[15], count_recv.at[15], twin)
    count_twin.start()
    halo_up = slab_copy(vol.at[ZL], vol.at[0], halo_send.at[0], halo_recv.at[0], above)
    halo_up.start()
    halo_down = slab_copy(vol.at[1], vol.at[ZL + 1], halo_send.at[1], halo_recv.at[1], below)
    halo_down.start()
    loads[2].wait()
    local_sums(1)
    pair_copy(1).start()

    def part_copies(part):
        return [
            slab_copy(
                pieces_[part].at[chip_at(d)], parts_[part].at[d],
                part_send.at[part, d], part_recv.at[part, d], 2 * chip_at(d) + core,
            )
            for d in range(15)
        ]

    def spread_pieces(part):
        _, keep, _ = half(part)
        n = PARTS[part][1] // 2
        pair_copy(part).wait()
        for j in range(CHIPS):
            r, c = n * (j // 2), BOX * (j % 2)
            pieces_[part][j] = (
                locals_[part][pl.ds(pl.multiple_of(keep + r, 8), n), c : c + BOX]
                + pairs[part][r : r + n, c : c + BOX]
            )
        for copy in part_copies(part):
            copy.start()

    def place(part, which):
        _, keep, _ = half(part)
        n = PARTS[part][1] // 2
        r = pl.multiple_of(keep + n * (which // 2), 8)
        c = pl.multiple_of(BOX * lax.rem(which, 2), 128)
        return pl.ds(r, n), pl.ds(c, BOX)

    def gather_copies(part):
        return [
            slab_copy(
                totals[part], sums[part].at[place(part, chip)],
                gather_send.at[part, d], gather_recv.at[part, d], 2 * chip_at(d) + core,
            )
            for d in range(15)
        ]

    def twin_copies(part, own=False):
        return [
            slab_copy(
                sums[part].at[place(part, w)], sums[part].at[place(part, w)],
                twin_send.at[part, d], twin_recv.at[part, d], twin,
            )
            for d, w in enumerate([chip_from(d) for d in range(15)] + ([chip] if own else []))
        ]

    def twin_own(part):
        spot = sums[part].at[place(part, chip)]
        return slab_copy(spot, spot, twin_send.at[part, 15], twin_recv.at[part, 15], twin)

    def add_pieces(part):
        total = pieces_[part][chip]
        for d, copy in enumerate(part_copies(part)):
            copy.wait()
            total = total + parts_[part][d]
        totals[part][...] = total
        for copy in gather_copies(part):
            copy.start()
        sums[part][place(part, chip)] = total
        twin_own(part).start()

    def forward_pieces(part):
        for gather, forward in list(zip(gather_copies(part), twin_copies(part)))[::-1]:
            gather.wait()
            forward.start()

    def take_sums(part):
        for copy in twin_copies(part, True):
            copy.wait()

    def project(part, o):
        y, n = PARTS[part]
        for h in range(2):
            cols = slice(h * BOX, (h + 1) * BOX)
            seen = jnp.dot(
                vol[:, y : y + n, cols].reshape((ZL + 2) * n, BOX), width[:, o * BOX : (o + 1) * BOX],
                preferred_element_type=F32,
            ).reshape(ZL + 2, n, BOX)
            total = jnp.zeros((n, BOX), F32)
            for j in range(ZL + 2):
                total = total + depth[o, j : j + 1, :] * seen[j]
            proj[o, y : y + n, cols] = total

    spread_pieces(0)
    plane = lax.broadcasted_iota(jnp.int32, (16, BOX), 0) + (me * ZL - 1)
    column = lax.broadcasted_iota(jnp.int32, (BOX, BOX), 0)
    for o in range(ORI):
        low, frac = interp_row(tz_ref[o])
        weights = jnp.where(plane == low, 1.0 - frac, 0.0) + jnp.where(plane == low + 1, frac, 0.0)
        depth[o] = jnp.where(plane < BOX, weights, 0.0)
        low, frac = interp_row(tx_ref[o])
        table = jnp.where(column == low, 1.0 - frac, 0.0) + jnp.where(column == low + 1, frac, 0.0)
        width[:, o * BOX : (o + 1) * BOX] = table.astype(BF16)

    count_twin.wait()
    count_buf[15] = count_own[...] + count_pair[...]
    counts = [
        slab_copy(count_buf.at[15], count_buf.at[d], count_send.at[d], count_recv.at[d], 2 * chip_at(d) + core)
        for d in range(15)
    ]
    for copy in counts:
        copy.start()
    halo_up.wait()
    halo_down.wait()
    spread_pieces(1)
    for o in range(ORI):
        project(0, o)
    add_pieces(0)

    def weigh(part):
        y, n = PARTS[part]
        ctf = ctf_buf[:, y : y + n, :].astype(F32)
        square = ctf * ctf
        for o in range(ORI):
            have = jnp.zeros((n, BOX), F32)
            for d in range(DEF):
                have = have + number[o : o + 1, d : d + 1] * square[d]
            power[o, y : y + n, :] = have
            k = slice(o * BOX, (o + 1) * BOX)
            for z in range(ZL):
                operand[z * n : (z + 1) * n, k] = (depth[o, z + 1 : z + 2, :] * have).astype(BF16)
        back = lax.dot_general(
            operand[: ZL * n, :], width[...], (((1,), (1,)), ((), ())), preferred_element_type=F32
        )
        weight[:, y : y + n, :] = back.reshape(ZL, n, BOX) + TAU

    number = count_buf[15]
    for d in range(15):
        counts[d].wait()
        number = number + count_buf[d]
    weigh(0)
    add_pieces(1)
    for o in range(3):
        project(1, o)
    forward_pieces(0)
    for o in range(3, 5):
        project(1, o)
    take_sums(0)
    loads[4].wait()

    def update(part, first, last):
        y, n = PARTS[part]
        count = last - first
        for o in range(ORI):
            k = slice(o * BOX, (o + 1) * BOX)
            for h in range(2):
                cols = slice(h * BOX, (h + 1) * BOX)
                numer = sums[part][o * n : (o + 1) * n, cols] - power[o, y : y + n, :] * proj[o, y : y + n, cols]
                for zi in range(count):
                    r = (zi * 2 + h) * n
                    w = depth[o, first + zi + 1 : first + zi + 2, :]
                    operand[r : r + n, k] = (w * numer).astype(BF16)
        m = count * 2 * n
        back = lax.dot_general(
            operand[:m, :], width[...], (((1,), (1,)), ((), ())), preferred_element_type=F32
        )
        for zi in range(count):
            z = first + zi
            fresh = []
            for h in range(2):
                r = (zi * 2 + h) * n
                old = vol[z + 1, y : y + n, h * BOX : (h + 1) * BOX].astype(F32)
                fresh.append((old + back[r : r + n] / weight[z, y : y + n, :]).astype(BF16))
            r = zi * 2 * n
            paired[r : r + n, :BOX] = fresh[0]
            paired[r : r + n, BOX:] = fresh[1]
            paired[r + n : r + 2 * n, :BOX] = fresh[1]
            paired[r + n : r + 2 * n, BOX:] = -fresh[0]
        return lax.dot_general(
            x_tab[...], paired[:m, :], (((1,), (1,)), ((), ())), preferred_element_type=F32
        ).astype(BF16).reshape(NB, XL, m)

    def batch_piece(c, d):
        to = lax.rem(row_block + d, NB)
        src = along0.at[to] if c == 0 else along1.at[c - 1, to]
        dst = pieces0.at[row_block] if c == 0 else pieces1.at[c - 1, row_block]
        return batch_copy(src, dst, batch_send.at[c, d], batch_recv.at[c, d], to)

    def batch_local(c):
        src = along0.at[row_block] if c == 0 else along1.at[c - 1, row_block]
        dst = pieces0.at[row_block] if c == 0 else pieces1.at[c - 1, row_block]
        return pltpu.make_async_copy(src, dst, batch_own.at[c])

    def batch_go(c):
        for d in (4, 3, 5, 2, 6, 1, 7):
            batch_piece(c, d).start()
        batch_local(c).start()

    def batch_done(c):
        for d in range(1, NB):
            batch_piece(c, d).wait()
        batch_local(c).wait()

    along0[...] = update(0, 0, ZL)
    batch_go(0)
    for o in range(5, ORI):
        project(1, o)
    weigh(1)
    forward_pieces(1)
    take_sums(1)
    for c in range(CH):
        along1[c] = update(1, c * ZC, (c + 1) * ZC)
        batch_go(c + 1)

    loads[5].wait()

    def slab_piece(g, d, e):
        lanes = pl.ds(GROUPS[g][0] * ZC * XL, (384, 256)[g])
        to = 2 * chip_at(d) + (core if e == 0 else 1 - core) if d < 15 else twin
        return slab_copy(
            along_y.at[to, :, lanes], landed.at[me, :, lanes], slab_send.at[g, 2 * d + e], slab_recv.at[g, 2 * d + e], to
        )

    def slab_local(g):
        lanes = pl.ds(GROUPS[g][0] * ZC * XL, (384, 256)[g])
        return pltpu.make_async_copy(along_y.at[me, :, lanes], landed.at[me, :, lanes], slab_own.at[g])

    targets = [(d, e) for d in range(15) for e in range(2)] + [(15, 0)]
    along_y[:, :, ZL * XL :] = jnp.zeros((NS, 2 * ZL, LANES - ZL * XL), BF16)
    wide0, wide1 = (2 * n for _, n in PARTS)
    batch_done(0)
    for z in range(ZL):
        gathered[z * XL : (z + 1) * XL, : NB * wide0] = jnp.concatenate(
            [pieces0[b, :, z * wide0 : (z + 1) * wide0] for b in range(NB)], axis=1
        )
    for g, (first, last) in enumerate(GROUPS):
        for c in range(first, last):
            batch_done(c + 1)
            for zi in range(ZC):
                z = c * ZC + zi
                gathered[z * XL : (z + 1) * XL, NB * wide0 :] = jnp.concatenate(
                    [pieces1[c, b, :, zi * wide1 : (zi + 1) * wide1] for b in range(NB)], axis=1
                )
        low, high = first * ZC * XL, last * ZC * XL
        out = lax.dot_general(
            y_tab[...], gathered[low:high, :], (((1,), (1,)), ((), ())), preferred_element_type=F32
        )
        along_y[:, :, low:high] = out.astype(BF16).reshape(NS, 2 * ZL, high - low)
        for d, e in targets:
            slab_piece(g, d, e).start()
        slab_local(g).start()
    stores = []
    for g in range(len(GROUPS)):
        for d, e in targets:
            slab_piece(g, d, e).wait()
        slab_local(g).wait()
        for t in ((0, 1, 2), (3, 4))[g]:
            wide[t] = landed[:, :, t * 128 : (t + 1) * 128].astype(F32).reshape(NS * 2 * ZL, 128)
        for z in range(GROUPS[g][0] * ZC, GROUPS[g][1] * ZC):
            t, off = z * XL // 128, z * XL % 128
            for h in range(2):
                blocks = []
                for y in range(ZL):
                    spot = pl.ds(h * ZL + y, NS, 2 * ZL)
                    if off + XL <= 128:
                        blocks.append(wide[t, spot, :][:, off : off + XL])
                    else:
                        both = jnp.concatenate([wide[t, spot, :], wide[t + 1, spot, :]], axis=1)
                        blocks.append(both[:, off : off + XL])
                r = (z * 2 + h) * NS
                turned[r : r + NS, :] = jnp.concatenate(blocks, axis=1).astype(BF16)
        done = pl.ds(GROUPS[g][0] * ZC * 2 * NS, (GROUPS[g][1] - GROUPS[g][0]) * ZC * 2 * NS)
        stores.append(pltpu.make_async_copy(turned.at[done], out_ref.at[done], store.at[g]))
        stores[g].start()
    for copy in stores:
        copy.wait()


def main(orient_ids, defocus_ids, tilt_z, tilt_x, images, volume, ctf_tables, x_tab, y_tab):
    dma = pltpu.SemaphoreType.DMA
    any_space = pl.BlockSpec(memory_space=pl.ANY)
    two = lambda shape, dtype: [pltpu.VMEM(shape(n), dtype) for _, n in PARTS]
    return pl.pallas_call(
        main_kernel,
        out_shape=jax.ShapeDtypeStruct((2 * BOX, ZL * XL), BF16),
        in_specs=[SMEM] * 4 + [any_space] * 5,
        out_specs=any_space,
        scratch_shapes=[
            *two(lambda n: (32, n, 2 * BOX), BF16),
            pltpu.VMEM((ZL + 2, YL, 2 * BOX), BF16),
            pltpu.VMEM((DEF, YL, BOX), BF16),
            pltpu.VMEM((BOX, 2 * BOX), BF16),
            pltpu.VMEM((2 * BOX, 2 * BOX), BF16),
            pltpu.VMEM((BOX, ORI * BOX), BF16),
            pltpu.VMEM((ORI, 16, BOX), F32),
            pltpu.VMEM((ORI, YL, 2 * BOX), F32),
            pltpu.VMEM((ORI, YL, BOX), F32),
            pltpu.VMEM((ZL * YL, ORI * BOX), BF16),
            pltpu.VMEM((ZL, YL, BOX), F32),
            pltpu.VMEM((BOX, 2 * BOX), BF16),
            *two(lambda n: (ORI * n, 2 * BOX), F32),
            *two(lambda n: (ORI * n // 2, 2 * BOX), F32),
            *two(lambda n: (CHIPS, n // 2, BOX), F32),
            *two(lambda n: (CHIPS - 1, n // 2, BOX), F32),
            *two(lambda n: (n // 2, BOX), F32),
            *two(lambda n: (ORI * n, 2 * BOX), F32),
            pltpu.VMEM((CHIPS, 8, 128), F32),
            pltpu.VMEM((8, 128), F32),
            pltpu.VMEM((8, 128), F32),
            pltpu.VMEM((NB, XL, ZL * 2 * PARTS[0][1]), BF16),
            pltpu.VMEM((CH, NB, XL, ZC * 2 * PARTS[1][1]), BF16),
            pltpu.VMEM((NB, XL, ZL * 2 * PARTS[0][1]), BF16),
            pltpu.VMEM((CH, NB, XL, ZC * 2 * PARTS[1][1]), BF16),
            pltpu.VMEM((ZL * XL, 2 * BOX), BF16),
            pltpu.VMEM((NS, 2 * ZL, LANES), BF16),
            pltpu.VMEM((NS, 2 * ZL, LANES), BF16),
            pltpu.VMEM((LANES // 128, NS * 2 * ZL, 128), F32),
            pltpu.VMEM((2 * BOX, ZL * XL), BF16),
            dma((6,)), dma((2,)), dma((2,)), dma((2, 15)), dma((2, 15)), dma((2, 15)), dma((2, 15)),
            dma((2, 16)), dma((2, 16)), dma((16,)), dma((16,)), dma((2,)), dma((2,)),
            dma((CH + 1, NB)), dma((CH + 1, NB)), dma((CH + 1,)), dma((2, 32)), dma((2, 32)), dma((2,)), dma((2,)),
        ],
        compiler_params=pltpu.CompilerParams(vmem_limit_bytes=LIMIT, collective_id=0, has_side_effects=True),
        name="main",
    )(orient_ids, defocus_ids, tilt_z, tilt_x, images, volume, ctf_tables, x_tab, y_tab)


def zpass_kernel(in_ref, ztab_ref, out_ref, x, tab, result, load, store):
    loads = [pltpu.make_async_copy(in_ref, x, load.at[2])] + [
        pltpu.make_async_copy(ztab_ref.at[:, pl.ds(h * BOX, BOX)], tab.at[h], load.at[h]) for h in range(2)
    ]
    for copy in loads:
        copy.start()
    loads[0].wait()
    stores = []
    for h in range(2):
        loads[h + 1].wait()
        result[h] = lax.dot_general(x[...], tab[h], (((0,), (0,)), ((), ())), preferred_element_type=F32)
        stores.append(pltpu.make_async_copy(result.at[h], out_ref.at[h], store.at[h]))
        stores[h].start()
    for copy in stores:
        copy.wait()


def zpass(x, z_tab):
    any_space = pl.BlockSpec(memory_space=pl.ANY)
    return pl.pallas_call(
        zpass_kernel,
        out_shape=jax.ShapeDtypeStruct((2, ZL * XL, BOX), F32),
        in_specs=[any_space] * 2,
        out_specs=any_space,
        scratch_shapes=[
            pltpu.VMEM((2 * BOX, ZL * XL), BF16),
            pltpu.VMEM((2, 2 * BOX, BOX), BF16),
            pltpu.VMEM((2, ZL * XL, BOX), F32),
            pltpu.SemaphoreType.DMA((3,)),
            pltpu.SemaphoreType.DMA((2,)),
        ],
        compiler_params=pltpu.CompilerParams(vmem_limit_bytes=LIMIT),
        name="zpass",
    )(x, z_tab)


def local(volume, images, orient_ids, defocus_ids, ctf_tables, tilt_z, tilt_x):
    x_tab, y_tab, z_tab = pass_tables()
    turned = main(orient_ids, defocus_ids, tilt_z, tilt_x, images, volume, ctf_tables, x_tab, y_tab)
    return zpass(turned, z_tab).reshape(2, ZL, XL, BOX)


def solution(mesh):
    in_specs = (
        P("slab", "batch", None),
        P("slab", "batch", None),
        P("slab"),
        P("slab"),
        P(None, "batch", None),
        P(),
        P(),
    )
    out_specs = P(None, "slab", "batch", None)
    return jax.shard_map(local, mesh=mesh, in_specs=in_specs, out_specs=out_specs, check_vma=False)
```

```python
import functools
import math

import jax
import jax.numpy as jnp
import numpy as np
from jax import lax
from jax.experimental import pallas as pl
from jax.experimental.pallas import tpu as pltpu
from jax.sharding import PartitionSpec as P

TAU = 1.0
BOX = 384
HALF = 192
ORI = 8
DEF = 8
NS = 32
NB = 8
ZL = BOX // NS
YL = BOX // NB
XL = BOX // NB
CH = 3
ZC = ZL // CH
PARTS = ((0, 16), (16, 32))
CHIPS = NS // 2
LANES = 640
F32 = jnp.float32
BF16 = jnp.bfloat16
VMEM = pl.BlockSpec(memory_space=pltpu.VMEM)
SMEM = pl.BlockSpec(memory_space=pltpu.SMEM)
LIMIT = 58 * 1024 * 1024


def dft_tables():
    index = np.arange(BOX, dtype=np.int64)
    phases = (index[:, None] * index[None, :] % BOX).astype(np.float64)
    angles = phases * (2.0 * math.pi / BOX)
    factor = 1.0 / math.sqrt(BOX)
    return np.cos(angles) * factor, np.sin(angles) * factor


def pass_tables():
    cos, sin = dft_tables()
    x_tab = np.concatenate([cos, -sin], axis=0).T
    full = np.stack([np.stack([cos, sin], 1), np.stack([-sin, cos], 1)], 0)
    split = full.reshape(2, NB, YL, 2, NS, ZL).transpose(4, 3, 5, 1, 0, 2)
    y_tab = np.concatenate(
        [split[..., y : y + n].reshape(2 * BOX, NB * 2 * n) for y, n in PARTS], axis=1
    )
    z_tab = full.reshape(2, NS, ZL, 2, BOX).transpose(2, 0, 1, 3, 4).reshape(2 * BOX, 2 * BOX)
    return tuple(jnp.asarray(t.astype(np.float32), F32).astype(BF16) for t in (x_tab, y_tab, z_tab))


def slab_copy(src, dst, send, recv, to):
    return pltpu.make_async_remote_copy(
        src_ref=src, dst_ref=dst, send_sem=send, recv_sem=recv,
        device_id={"slab": to}, device_id_type=pl.DeviceIdType.MESH,
    )


def batch_copy(src, dst, send, recv, to):
    return pltpu.make_async_remote_copy(
        src_ref=src, dst_ref=dst, send_sem=send, recv_sem=recv,
        device_id={"batch": to}, device_id_type=pl.DeviceIdType.MESH,
    )


def interp_row(tilt):
    column = lax.broadcasted_iota(jnp.int32, (1, BOX), 1)
    position = HALF * 256 + (column - HALF) * tilt
    low = position >> 8
    fraction = (position & 255).astype(F32) * (1.0 / 256.0)
    return low, fraction


OFFSETS = [(2, 2), (3, 2), (2, 3), (1, 2), (2, 1), (0, 2), (2, 0), (3, 1), (1, 3), (3, 3), (1, 1), (0, 3), (0, 1), (3, 0), (1, 0)]
GROUPS = ((0, 2), (2, 3))


def main_kernel(
    orient_ref, defocus_ref, tz_ref, tx_ref, image_ref, volume_ref, ctf_ref, xtab_ref, ytab_ref,
    out_ref,
    image0, image1, vol, ctf_buf, x_tab, y_tab, width, depth, proj, power, operand, weight, paired,
    local0, local1, pair0, pair1, piece0, piece1, part0, part1, total0, total1, sums0, sums1,
    count_buf, count_pair, count_own,
    along0, along1, pieces0, pieces1, gathered, along_y, landed, wide, turned,
    load, pair_send, pair_recv, part_send, part_recv, gather_send, gather_recv, twin_send, twin_recv,
    count_send, count_recv, halo_send, halo_recv, batch_send, batch_recv, batch_own, slab_send, slab_recv, slab_own, store,
):
    me = lax.axis_index("slab")
    row_block = lax.axis_index("batch")
    core = lax.rem(me, 2)
    chip = me // 2
    chip_x = lax.rem(chip, 4)
    chip_y = chip // 4
    twin = me + 1 - 2 * core
    below = lax.rem(me + NS - 1, NS)
    above = lax.rem(me + 1, NS)
    images, locals_, pairs = (image0, image1), (local0, local1), (pair0, pair1)
    pieces_, parts_, totals, sums = (piece0, piece1), (part0, part1), (total0, total1), (sums0, sums1)

    def chip_at(d):
        x, y = OFFSETS[d]
        return 4 * lax.rem(chip_y + y, 4) + lax.rem(chip_x + x, 4)

    def chip_from(d):
        x, y = OFFSETS[d]
        return 4 * lax.rem(chip_y + 4 - y, 4) + lax.rem(chip_x + 4 - x, 4)

    mesh_id = pl.DeviceIdType.MESH
    barrier = pltpu.get_barrier_semaphore()

    def greet(d, _):
        pl.semaphore_signal(barrier, inc=1, device_id={"slab": lax.rem(me + d, NS)}, device_id_type=mesh_id)
        return 0

    lax.fori_loop(1, NS, greet, 0)

    def greet_batch(d, _):
        pl.semaphore_signal(barrier, inc=1, device_id={"batch": lax.rem(row_block + d, NB)}, device_id_type=mesh_id)
        return 0

    lax.fori_loop(1, NB, greet_batch, 0)

    loads = [
        pltpu.make_async_copy(src, dst, load.at[i])
        for i, (src, dst) in enumerate([
            (ctf_ref, ctf_buf),
            (image_ref.at[:, pl.ds(PARTS[0][0], PARTS[0][1])], image0),
            (image_ref.at[:, pl.ds(PARTS[1][0], PARTS[1][1])], image1),
            (volume_ref, vol.at[pl.ds(1, ZL)]),
            (xtab_ref, x_tab),
            (ytab_ref, y_tab),
        ])
    ]
    for copy in loads:
        copy.start()

    def local_sums(part):
        for r in range(0, PARTS[part][1], 16):
            for t in range(0, BOX, 128):
                def step(p, totals_):
                    orient, defocus = orient_ref[p], defocus_ref[p]
                    ctf = ctf_buf[defocus, PARTS[part][0] + r : PARTS[part][0] + r + 16, t : t + 128].astype(F32)
                    terms = [
                        ctf * images[part][p, r : r + 16, h * BOX + t : h * BOX + t + 128].astype(F32) for h in range(2)
                    ]
                    hot = [jnp.where(orient == o, 1.0, 0.0) for o in range(ORI)]
                    return tuple(totals_[2 * o + h] + hot[o] * terms[h] for o in range(ORI) for h in range(2))

                have = lax.fori_loop(0, 32, step, tuple(jnp.zeros((16, 128), F32) for _ in range(2 * ORI)), unroll=4)
                for o in range(ORI):
                    for h in range(2):
                        row = o * PARTS[part][1] + r
                        locals_[part][row : row + 16, h * BOX + t : h * BOX + t + 128] = have[2 * o + h]

    loads[0].wait()
    loads[1].wait()
    local_sums(0)
    row = lax.broadcasted_iota(jnp.int32, (8, 128), 0)
    lane = lax.broadcasted_iota(jnp.int32, (8, 128), 1)

    def count_step(p, have):
        return have + jnp.where((row == orient_ref[p]) & (lane == defocus_ref[p]), 1.0, 0.0)

    count_own[...] = lax.fori_loop(0, 32, count_step, jnp.zeros((8, 128), F32), unroll=4)
    loads[3].wait()

    pl.semaphore_wait(barrier, NS + NB - 2)

    def half(part):
        rows = ORI * PARTS[part][1] // 2
        return rows, pl.multiple_of(rows * core, rows), pl.multiple_of(rows * (1 - core), rows)

    def pair_copy(part):
        rows, _, give = half(part)
        return slab_copy(
            locals_[part].at[pl.ds(give, rows)], pairs[part], pair_send.at[part], pair_recv.at[part], twin
        )

    pair_copy(0).start()
    count_twin = slab_copy(count_own, count_pair, count_send.at[15], count_recv.at[15], twin)
    count_twin.start()
    halo_up = slab_copy(vol.at[ZL], vol.at[0], halo_send.at[0], halo_recv.at[0], above)
    halo_up.start()
    halo_down = slab_copy(vol.at[1], vol.at[ZL + 1], halo_send.at[1], halo_recv.at[1], below)
    halo_down.start()
    loads[2].wait()
    local_sums(1)
    pair_copy(1).start()

    def part_copies(part):
        return [
            slab_copy(
                pieces_[part].at[chip_at(d)], parts_[part].at[d],
                part_send.at[part, d], part_recv.at[part, d], 2 * chip_at(d) + core,
            )
            for d in range(15)
        ]

    def spread_pieces(part):
        _, keep, _ = half(part)
        n = PARTS[part][1] // 2
        pair_copy(part).wait()
        for j in range(CHIPS):
            r, c = n * (j // 2), BOX * (j % 2)
            pieces_[part][j] = (
                locals_[part][pl.ds(pl.multiple_of(keep + r, 8), n), c : c + BOX]
                + pairs[part][r : r + n, c : c + BOX]
            )
        for copy in part_copies(part):
            copy.start()

    def place(part, which):
        _, keep, _ = half(part)
        n = PARTS[part][1] // 2
        r = pl.multiple_of(keep + n * (which // 2), 8)
        c = pl.multiple_of(BOX * lax.rem(which, 2), 128)
        return pl.ds(r, n), pl.ds(c, BOX)

    def gather_copies(part):
        return [
            slab_copy(
                totals[part], sums[part].at[place(part, chip)],
                gather_send.at[part, d], gather_recv.at[part, d], 2 * chip_at(d) + core,
            )
            for d in range(15)
        ]

    def twin_copies(part, own=False):
        return [
            slab_copy(
                sums[part].at[place(part, w)], sums[part].at[place(part, w)],
                twin_send.at[part, d], twin_recv.at[part, d], twin,
            )
            for d, w in enumerate([chip_from(d) for d in range(15)] + ([chip] if own else []))
        ]

    def twin_own(part):
        spot = sums[part].at[place(part, chip)]
        return slab_copy(spot, spot, twin_send.at[part, 15], twin_recv.at[part, 15], twin)

    def add_pieces(part):
        total = pieces_[part][chip]
        for d, copy in enumerate(part_copies(part)):
            copy.wait()
            total = total + parts_[part][d]
        totals[part][...] = total
        for copy in gather_copies(part):
            copy.start()
        sums[part][place(part, chip)] = total
        twin_own(part).start()

    def forward_pieces(part):
        for gather, forward in list(zip(gather_copies(part), twin_copies(part)))[::-1]:
            gather.wait()
            forward.start()

    def take_sums(part):
        for copy in twin_copies(part, True):
            copy.wait()

    def project(part, o):
        y, n = PARTS[part]
        for h in range(2):
            cols = slice(h * BOX, (h + 1) * BOX)
            seen = jnp.dot(
                vol[:, y : y + n, cols].reshape((ZL + 2) * n, BOX), width[:, o * BOX : (o + 1) * BOX],
                preferred_element_type=F32,
            ).reshape(ZL + 2, n, BOX)
            total = jnp.zeros((n, BOX), F32)
            for j in range(ZL + 2):
                total = total + depth[o, j : j + 1, :] * seen[j]
            proj[o, y : y + n, cols] = total

    spread_pieces(0)
    plane = lax.broadcasted_iota(jnp.int32, (16, BOX), 0) + (me * ZL - 1)
    column = lax.broadcasted_iota(jnp.int32, (BOX, BOX), 0)
    for o in range(ORI):
        low, frac = interp_row(tz_ref[o])
        weights = jnp.where(plane == low, 1.0 - frac, 0.0) + jnp.where(plane == low + 1, frac, 0.0)
        depth[o] = jnp.where(plane < BOX, weights, 0.0)
        low, frac = interp_row(tx_ref[o])
        table = jnp.where(column == low, 1.0 - frac, 0.0) + jnp.where(column == low + 1, frac, 0.0)
        width[:, o * BOX : (o + 1) * BOX] = table.astype(BF16)

    count_twin.wait()
    count_buf[15] = count_own[...] + count_pair[...]
    counts = [
        slab_copy(count_buf.at[15], count_buf.at[d], count_send.at[d], count_recv.at[d], 2 * chip_at(d) + core)
        for d in range(15)
    ]
    for copy in counts:
        copy.start()
    halo_up.wait()
    halo_down.wait()
    spread_pieces(1)
    for o in range(ORI):
        project(0, o)
    add_pieces(0)

    def weigh(part):
        y, n = PARTS[part]
        ctf = ctf_buf[:, y : y + n, :].astype(F32)
        square = ctf * ctf
        for o in range(ORI):
            have = jnp.zeros((n, BOX), F32)
            for d in range(DEF):
                have = have + number[o : o + 1, d : d + 1] * square[d]
            power[o, y : y + n, :] = have
            k = slice(o * BOX, (o + 1) * BOX)
            for z in range(ZL):
                operand[z * n : (z + 1) * n, k] = (depth[o, z + 1 : z + 2, :] * have).astype(BF16)
        back = lax.dot_general(
            operand[: ZL * n, :], width[...], (((1,), (1,)), ((), ())), preferred_element_type=F32
        )
        weight[:, y : y + n, :] = back.reshape(ZL, n, BOX) + TAU

    number = count_buf[15]
    for d in range(15):
        counts[d].wait()
        number = number + count_buf[d]
    weigh(0)
    add_pieces(1)
    for o in range(3):
        project(1, o)
    forward_pieces(0)
    for o in range(3, 5):
        project(1, o)
    take_sums(0)
    loads[4].wait()

    def update(part, first, last):
        y, n = PARTS[part]
        count = last - first
        for o in range(ORI):
            k = slice(o * BOX, (o + 1) * BOX)
            for h in range(2):
                cols = slice(h * BOX, (h + 1) * BOX)
                numer = sums[part][o * n : (o + 1) * n, cols] - power[o, y : y + n, :] * proj[o, y : y + n, cols]
                for zi in range(count):
                    r = (zi * 2 + h) * n
                    w = depth[o, first + zi + 1 : first + zi + 2, :]
                    operand[r : r + n, k] = (w * numer).astype(BF16)
        m = count * 2 * n
        back = lax.dot_general(
            operand[:m, :], width[...], (((1,), (1,)), ((), ())), preferred_element_type=F32
        )
        for zi in range(count):
            z = first + zi
            fresh = []
            for h in range(2):
                r = (zi * 2 + h) * n
                old = vol[z + 1, y : y + n, h * BOX : (h + 1) * BOX].astype(F32)
                fresh.append((old + back[r : r + n] / weight[z, y : y + n, :]).astype(BF16))
            r = zi * 2 * n
            paired[r : r + n, :BOX] = fresh[0]
            paired[r : r + n, BOX:] = fresh[1]
            paired[r + n : r + 2 * n, :BOX] = fresh[1]
            paired[r + n : r + 2 * n, BOX:] = -fresh[0]
        return lax.dot_general(
            x_tab[...], paired[:m, :], (((1,), (1,)), ((), ())), preferred_element_type=F32
        ).astype(BF16).reshape(NB, XL, m)

    def batch_ends(c, src, dst):
        if c in (0, CH + 1):
            lanes = pl.ds(0, 256) if c == 0 else pl.ds(256, 128)
            return along0.at[src, :, lanes], pieces0.at[dst, :, lanes]
        return along1.at[c - 1, src], pieces1.at[c - 1, dst]

    def batch_piece(c, d):
        to = lax.rem(row_block + d, NB)
        src, dst = batch_ends(c, to, row_block)
        return batch_copy(src, dst, batch_send.at[c, d], batch_recv.at[c, d], to)

    def batch_local(c):
        src, dst = batch_ends(c, row_block, row_block)
        return pltpu.make_async_copy(src, dst, batch_own.at[c])

    def batch_go(c):
        for d in (4, 3, 5, 2, 6, 1, 7):
            batch_piece(c, d).start()
        batch_local(c).start()

    def batch_done(c):
        for d in range(1, NB):
            batch_piece(c, d).wait()
        batch_local(c).wait()

    along0[:, :, :256] = update(0, 0, 8)
    batch_go(0)
    for o in range(5, 7):
        project(1, o)
    forward_pieces(1)
    project(1, 7)
    weigh(1)
    take_sums(1)
    for c in range(CH):
        along1[c] = update(1, c * ZC, (c + 1) * ZC)
        batch_go(c + 1)
        if c == 1:
            along0[:, :, 256:] = update(0, 8, ZL)
            batch_go(CH + 1)

    loads[5].wait()

    def slab_piece(g, d, e):
        lanes = pl.ds(GROUPS[g][0] * ZC * XL, (384, 256)[g])
        to = 2 * chip_at(d) + (core if e == 0 else 1 - core) if d < 15 else twin
        return slab_copy(
            along_y.at[to, :, lanes], landed.at[me, :, lanes], slab_send.at[g, 2 * d + e], slab_recv.at[g, 2 * d + e], to
        )

    def slab_local(g):
        lanes = pl.ds(GROUPS[g][0] * ZC * XL, (384, 256)[g])
        return pltpu.make_async_copy(along_y.at[me, :, lanes], landed.at[me, :, lanes], slab_own.at[g])

    targets = [(d, e) for d in range(15) for e in range(2)] + [(15, 0)]
    along_y[:, :, ZL * XL :] = jnp.zeros((NS, 2 * ZL, LANES - ZL * XL), BF16)
    wide0, wide1 = (2 * n for _, n in PARTS)
    def take_first(low, high):
        for z in range(low, high):
            gathered[z * XL : (z + 1) * XL, : NB * wide0] = jnp.concatenate(
                [pieces0[b, :, z * wide0 : (z + 1) * wide0] for b in range(NB)], axis=1
            )

    for g, (first, last) in enumerate(GROUPS):
        batch_done((0, CH + 1)[g])
        take_first(first * ZC, last * ZC)
        for c in range(first, last):
            batch_done(c + 1)
            for zi in range(ZC):
                z = c * ZC + zi
                gathered[z * XL : (z + 1) * XL, NB * wide0 :] = jnp.concatenate(
                    [pieces1[c, b, :, zi * wide1 : (zi + 1) * wide1] for b in range(NB)], axis=1
                )
        low, high = first * ZC * XL, last * ZC * XL
        out = lax.dot_general(
            y_tab[...], gathered[low:high, :], (((1,), (1,)), ((), ())), preferred_element_type=F32
        )
        along_y[:, :, low:high] = out.astype(BF16).reshape(NS, 2 * ZL, high - low)
        for d, e in targets:
            slab_piece(g, d, e).start()
        slab_local(g).start()
    stores = []
    for g in range(len(GROUPS)):
        for d, e in targets:
            slab_piece(g, d, e).wait()
        slab_local(g).wait()
        for t in ((0, 1, 2), (3, 4))[g]:
            wide[t] = landed[:, :, t * 128 : (t + 1) * 128].astype(F32).reshape(NS * 2 * ZL, 128)
        for z in range(GROUPS[g][0] * ZC, GROUPS[g][1] * ZC):
            t, off = z * XL // 128, z * XL % 128
            for h in range(2):
                blocks = []
                for y in range(ZL):
                    spot = pl.ds(h * ZL + y, NS, 2 * ZL)
                    if off + XL <= 128:
                        blocks.append(wide[t, spot, :][:, off : off + XL])
                    else:
                        both = jnp.concatenate([wide[t, spot, :], wide[t + 1, spot, :]], axis=1)
                        blocks.append(both[:, off : off + XL])
                r = (z * 2 + h) * NS
                turned[r : r + NS, :] = jnp.concatenate(blocks, axis=1).astype(BF16)
        done = pl.ds(GROUPS[g][0] * ZC * 2 * NS, (GROUPS[g][1] - GROUPS[g][0]) * ZC * 2 * NS)
        stores.append(pltpu.make_async_copy(turned.at[done], out_ref.at[done], store.at[g]))
        stores[g].start()
    for copy in stores:
        copy.wait()


def main(orient_ids, defocus_ids, tilt_z, tilt_x, images, volume, ctf_tables, x_tab, y_tab):
    dma = pltpu.SemaphoreType.DMA
    any_space = pl.BlockSpec(memory_space=pl.ANY)
    two = lambda shape, dtype: [pltpu.VMEM(shape(n), dtype) for _, n in PARTS]
    return pl.pallas_call(
        main_kernel,
        out_shape=jax.ShapeDtypeStruct((2 * BOX, ZL * XL), BF16),
        in_specs=[SMEM] * 4 + [any_space] * 5,
        out_specs=any_space,
        scratch_shapes=[
            *two(lambda n: (32, n, 2 * BOX), BF16),
            pltpu.VMEM((ZL + 2, YL, 2 * BOX), BF16),
            pltpu.VMEM((DEF, YL, BOX), BF16),
            pltpu.VMEM((BOX, 2 * BOX), BF16),
            pltpu.VMEM((2 * BOX, 2 * BOX), BF16),
            pltpu.VMEM((BOX, ORI * BOX), BF16),
            pltpu.VMEM((ORI, 16, BOX), F32),
            pltpu.VMEM((ORI, YL, 2 * BOX), F32),
            pltpu.VMEM((ORI, YL, BOX), F32),
            pltpu.VMEM((ZL * YL, ORI * BOX), BF16),
            pltpu.VMEM((ZL, YL, BOX), F32),
            pltpu.VMEM((BOX, 2 * BOX), BF16),
            *two(lambda n: (ORI * n, 2 * BOX), F32),
            *two(lambda n: (ORI * n // 2, 2 * BOX), F32),
            *two(lambda n: (CHIPS, n // 2, BOX), F32),
            *two(lambda n: (CHIPS - 1, n // 2, BOX), F32),
            *two(lambda n: (n // 2, BOX), F32),
            *two(lambda n: (ORI * n, 2 * BOX), F32),
            pltpu.VMEM((CHIPS, 8, 128), F32),
            pltpu.VMEM((8, 128), F32),
            pltpu.VMEM((8, 128), F32),
            pltpu.VMEM((NB, XL, ZL * 2 * PARTS[0][1]), BF16),
            pltpu.VMEM((CH, NB, XL, ZC * 2 * PARTS[1][1]), BF16),
            pltpu.VMEM((NB, XL, ZL * 2 * PARTS[0][1]), BF16),
            pltpu.VMEM((CH, NB, XL, ZC * 2 * PARTS[1][1]), BF16),
            pltpu.VMEM((ZL * XL, 2 * BOX), BF16),
            pltpu.VMEM((NS, 2 * ZL, LANES), BF16),
            pltpu.VMEM((NS, 2 * ZL, LANES), BF16),
            pltpu.VMEM((LANES // 128, NS * 2 * ZL, 128), F32),
            pltpu.VMEM((2 * BOX, ZL * XL), BF16),
            dma((6,)), dma((2,)), dma((2,)), dma((2, 15)), dma((2, 15)), dma((2, 15)), dma((2, 15)),
            dma((2, 16)), dma((2, 16)), dma((16,)), dma((16,)), dma((2,)), dma((2,)),
            dma((CH + 2, NB)), dma((CH + 2, NB)), dma((CH + 2,)), dma((2, 32)), dma((2, 32)), dma((2,)), dma((2,)),
        ],
        compiler_params=pltpu.CompilerParams(vmem_limit_bytes=LIMIT, collective_id=0, has_side_effects=True),
        name="main",
    )(orient_ids, defocus_ids, tilt_z, tilt_x, images, volume, ctf_tables, x_tab, y_tab)


def zpass_kernel(in_ref, ztab_ref, out_ref, x, tab, result, load, store):
    loads = [pltpu.make_async_copy(in_ref, x, load.at[2])] + [
        pltpu.make_async_copy(ztab_ref.at[:, pl.ds(h * BOX, BOX)], tab.at[h], load.at[h]) for h in range(2)
    ]
    for copy in loads:
        copy.start()
    loads[0].wait()
    stores = []
    for h in range(2):
        loads[h + 1].wait()
        result[h] = lax.dot_general(x[...], tab[h], (((0,), (0,)), ((), ())), preferred_element_type=F32)
        stores.append(pltpu.make_async_copy(result.at[h], out_ref.at[h], store.at[h]))
        stores[h].start()
    for copy in stores:
        copy.wait()


def zpass(x, z_tab):
    any_space = pl.BlockSpec(memory_space=pl.ANY)
    return pl.pallas_call(
        zpass_kernel,
        out_shape=jax.ShapeDtypeStruct((2, ZL * XL, BOX), F32),
        in_specs=[any_space] * 2,
        out_specs=any_space,
        scratch_shapes=[
            pltpu.VMEM((2 * BOX, ZL * XL), BF16),
            pltpu.VMEM((2, 2 * BOX, BOX), BF16),
            pltpu.VMEM((2, ZL * XL, BOX), F32),
            pltpu.SemaphoreType.DMA((3,)),
            pltpu.SemaphoreType.DMA((2,)),
        ],
        compiler_params=pltpu.CompilerParams(vmem_limit_bytes=LIMIT),
        name="zpass",
    )(x, z_tab)


def local(volume, images, orient_ids, defocus_ids, ctf_tables, tilt_z, tilt_x):
    x_tab, y_tab, z_tab = pass_tables()
    turned = main(orient_ids, defocus_ids, tilt_z, tilt_x, images, volume, ctf_tables, x_tab, y_tab)
    return zpass(turned, z_tab).reshape(2, ZL, XL, BOX)


def solution(mesh):
    in_specs = (
        P("slab", "batch", None),
        P("slab", "batch", None),
        P("slab"),
        P("slab"),
        P(None, "batch", None),
        P(),
        P(),
    )
    out_specs = P(None, "slab", "batch", None)
    return jax.shard_map(local, mesh=mesh, in_specs=in_specs, out_specs=out_specs, check_vma=False)
```
